256 devices in a mesh: sim: 8 (over z_hi, y), slab: 32 (over z_lo, x, core).
Axes of the slice: x: 4, y: 4, z: 8 (z_hi: 2, z_lo: 4; z = z_hi * 4 + z_lo), core: 2. Of those that a mesh axis runs over, the one named last changes fastest.
Arguments:
- velocity: float32 [8, 3, 256, 256, 128], P('sim', None, None, 'slab'), may hold values from -3 to 5
- viscosity: float32 [8, 256, 256, 128], P('sim', None, 'slab'), may hold values from 0.02 to 0.12
- turbines: int32 [8, 256, 256, 128], P('sim', None, 'slab'), may hold values from 0 to 1, as said below
- fringe_start: int32 [1], replicated, may hold values from 0 to 224
Outputs:
- projected: float32 [8, 3, 256, 256, 128], P('sim', None, None, 'slab')
The draws below stay inside these ranges and needn't reach their ends.
Inputs may be any that keep to these rules, and one draw needn't show every extreme that they name: `turbines`: group 0, the precursor, holds no turbine cells.
All inputs are finite; a program needn't handle non-finite values.
Results may differ from the reference program's by a relative error of at most 0.0003.
Values sent between devices are 32-bit elements; how exact they have to be, the bound alone decides.
No kernel may reach another device: no remote copies, remote signals or barrier semaphores. Data moves between devices by JAX's collectives and lax.ppermute only.
A program may use at most 128 MiB of HBM per device.

```python
import math
import jax
import jax.numpy as jnp
from jax import lax

NX = 256
NY = 256
NZ = 128
FR = 32
STEPS = 1
GROUPS = 8


def draw_velocity(key, part):
    noise_key = jax.random.fold_in(jax.random.fold_in(key, 11), 0)
    full_shape = (GROUPS, 3, NX, NY, NZ)
    turbulence = jax.random.normal(noise_key, full_shape, jnp.float32)
    mean_flow = jnp.array([1.0, 0.0, 0.0], jnp.float32).reshape(1, 3, 1, 1, 1)
    values = 0.5 * turbulence + mean_flow
    return jnp.clip(values, -3.0, 5.0)


def draw_turbines(key, part):
    key_x, key_y, key_z = jax.random.split(jax.random.fold_in(key, 23), 3)
    machines = 12
    column_x = jax.random.randint(key_x, (GROUPS, machines), 0, NX)
    column_y = jax.random.randint(key_y, (GROUPS, machines), 0, NY)
    height_z = jax.random.randint(key_z, (GROUPS, machines), NZ // 4, NZ // 2 + 1)
    radius = max(NZ // 8, 1)
    along_x = jnp.arange(NX, dtype=jnp.int32).reshape(1, NX, 1, 1)
    along_y = jnp.arange(NY, dtype=jnp.int32).reshape(1, 1, NY, 1)
    along_z = jnp.arange(NZ, dtype=jnp.int32).reshape(1, 1, 1, NZ)
    disc_mask = jnp.zeros((GROUPS, NX, NY, NZ), jnp.int32)
    for machine in range(machines):
        centre_x = column_x[:, machine].reshape(GROUPS, 1, 1, 1)
        centre_y = column_y[:, machine].reshape(GROUPS, 1, 1, 1)
        centre_z = height_z[:, machine].reshape(GROUPS, 1, 1, 1)
        inside = (along_x == centre_x) & ((along_y - centre_y) ** 2 + (along_z - centre_z) ** 2 <= radius * radius)
        disc_mask = jnp.maximum(disc_mask, inside.astype(jnp.int32))
    group_ids = jnp.arange(GROUPS, dtype=jnp.int32).reshape(GROUPS, 1, 1, 1)
    return jnp.where(group_ids == 0, 0, disc_mask)


def steps_of(stream_key, dims, cuts, smallest, top_value):
    loudness = 1.0
    for axis_at, shards_of in cuts:
        draws = jax.random.uniform(jax.random.fold_in(jax.random.fold_in(stream_key, 6), axis_at), (shards_of,), jnp.float32, smallest / len(cuts), top_value / len(cuts))
        loudness = loudness * jnp.repeat(jnp.exp(draws), dims[axis_at] // shards_of).reshape((-1,) + (1,) * (len(dims) - 1 - axis_at))
    return loudness


def setup_inputs(seed: int = 0) -> dict:
    keys = jax.random.split(jax.random.key(seed), 5)
    velocity = draw_velocity(jax.random.fold_in(keys[4], 71), 0)
    viscosity = jnp.clip(jnp.exp(math.log(0.12) - 1.7917595 * jax.random.uniform(keys[1], (GROUPS, NX, NY, NZ), jnp.float32) ** steps_of(keys[1], (GROUPS, NX, NY, NZ), ((0, 8), (2, 32)), -0.2, 0.2)), 0.02, 0.12)
    turbines = draw_turbines(jax.random.fold_in(keys[4], 71), 0)
    fringe_start = jax.random.randint(keys[3], (1,), 0, NX - FR + 1).astype(jnp.int32)
    return dict(velocity=velocity, viscosity=viscosity, turbines=turbines, fringe_start=fringe_start)


highest = lax.Precision.HIGHEST
thrust_coef = 0.75


def wrap_y(values):
    return jnp.concatenate([values[..., -1:, :], values, values[..., :1, :]], -2)


def diffuse(fields, viscous):
    faces_x = 0.5 * (viscous + jnp.roll(viscous, -1, -3))
    flux_x = faces_x * (jnp.roll(fields, -1, -3) - fields)
    across_x = flux_x - jnp.roll(flux_x, 1, -3)
    faces_y = 0.5 * (viscous[..., 1:, :] + viscous[..., :-1, :])
    flux_y = faces_y * (fields[..., 1:, :] - fields[..., :-1, :])
    across_y = flux_y[..., 1:, :] - flux_y[..., :-1, :]
    faces_z = 0.5 * (viscous[..., 1:] + viscous[..., :-1])
    flux_z = faces_z * (fields[..., 1:] - fields[..., :-1])
    nothing = jnp.zeros_like(flux_z[..., :1])
    upper_flux = jnp.concatenate([flux_z, nothing], -1)
    lower_flux = jnp.concatenate([nothing, flux_z], -1)
    across_z = upper_flux - lower_flux
    return fields[..., 1:-1, :] + across_x[..., 1:-1, :] + across_y + across_z[..., 1:-1, :]


def drag(fields, turbine_cells):
    streamwise = fields[0]
    disc_mask = turbine_cells.astype(jnp.float32)
    streamwise = streamwise - 0.5 * thrust_coef * disc_mask * streamwise * jnp.abs(streamwise)
    return jnp.concatenate([streamwise[None], fields[1:]], 0)


def blend_rows(fields, precursor, first_row, active):
    length = precursor.shape[1]
    slab_rows = lax.dynamic_slice_in_dim(fields, first_row, length, 1)
    profile = jnp.sin(math.pi * (jnp.arange(length, dtype=jnp.float32) + 0.5) / length) ** 2 * active
    new_rows = slab_rows + profile[None, :, None, None] * (precursor - slab_rows)
    return lax.dynamic_update_slice_in_dim(fields, new_rows, first_row, 1)


def centered_x(values):
    return 0.5 * (jnp.roll(values, -1, -3) - jnp.roll(values, 1, -3))


def centered_y(extended):
    return 0.5 * (extended[..., 2:, :] - extended[..., :-2, :])


def centered_z(values):
    padded = jnp.concatenate([values[..., :1], values, values[..., -1:]], -1)
    return 0.5 * (padded[..., 2:] - padded[..., :-2])


def dft_tables(length):
    index_a = jnp.arange(length, dtype=jnp.int32)
    product = (index_a[:, None] * index_a[None, :]) % length
    angles = (2.0 * math.pi / length) * product.astype(jnp.float32)
    return jnp.cos(angles), jnp.sin(angles)


def dct_table(length):
    index_m = jnp.arange(length, dtype=jnp.int32)
    product = (index_m[:, None] * (2 * index_m[None, :] + 1)) % (4 * length)
    angles = (math.pi / (2.0 * length)) * product.astype(jnp.float32)
    return jnp.cos(angles)


def inverse_eigen(wave_x, wave_y, wave_z, length_x, length_y, length_z):
    eigen_x = 2.0 * jnp.cos(2.0 * math.pi * wave_x.astype(jnp.float32) / length_x) - 2.0
    eigen_y = 2.0 * jnp.cos(2.0 * math.pi * wave_y.astype(jnp.float32) / length_y) - 2.0
    eigen_z = 2.0 * jnp.cos(math.pi * wave_z.astype(jnp.float32) / length_z) - 2.0
    eigen_sum = eigen_x[:, None, None] + eigen_y[None, :, None] + eigen_z[None, None, :]
    zero_mode = (wave_x[:, None, None] == 0) & (wave_y[None, :, None] == 0) & (wave_z[None, None, :] == 0)
    guarded = jnp.where(zero_mode, 1.0, eigen_sum)
    return jnp.where(zero_mode, 0.0, 1.0 / guarded)


def poisson(source):
    cos_x, sin_x = dft_tables(NX)
    cos_y, sin_y = dft_tables(NY)
    cos_z = dct_table(NZ)
    z_modes = jnp.einsum("xyn,mn->xym", source, cos_z, precision=highest)
    real_part = jnp.einsum("kx,xyz->kyz", cos_x, z_modes, precision=highest)
    imag_part = -jnp.einsum("kx,xyz->kyz", sin_x, z_modes, precision=highest)
    y_real = jnp.einsum("ky,xyz->xkz", cos_y, real_part, precision=highest) + jnp.einsum("ky,xyz->xkz", sin_y, imag_part, precision=highest)
    y_imag = jnp.einsum("ky,xyz->xkz", cos_y, imag_part, precision=highest) - jnp.einsum("ky,xyz->xkz", sin_y, real_part, precision=highest)
    inverse = inverse_eigen(jnp.arange(NX, dtype=jnp.int32), jnp.arange(NY, dtype=jnp.int32), jnp.arange(NZ, dtype=jnp.int32), NX, NY, NZ)
    press_real = y_real * inverse
    press_imag = y_imag * inverse
    back_real = (jnp.einsum("ky,xyz->xkz", cos_y, press_real, precision=highest) - jnp.einsum("ky,xyz->xkz", sin_y, press_imag, precision=highest)) / NY
    back_imag = (jnp.einsum("ky,xyz->xkz", sin_y, press_real, precision=highest) + jnp.einsum("ky,xyz->xkz", cos_y, press_imag, precision=highest)) / NY
    spatial_x = (jnp.einsum("xk,kyz->xyz", cos_x, back_real, precision=highest) - jnp.einsum("xk,kyz->xyz", sin_x, back_imag, precision=highest)) / NX
    weights = jnp.where(jnp.arange(NZ, dtype=jnp.int32) == 0, 1.0, 2.0) / NZ
    return jnp.einsum("xym,mn->xyn", spatial_x, cos_z * weights[:, None], precision=highest)


def reference(velocity, viscosity, turbines, fringe_start):
    first_row = fringe_start[0]
    precursor = lax.dynamic_slice_in_dim(velocity[0], first_row, FR, 1)

    def one_group(group_index):
        fields = velocity[group_index]
        viscous = viscosity[group_index]
        for substep in range(STEPS):
            fields = diffuse(wrap_y(fields), wrap_y(viscous))
        fields = drag(fields, turbines[group_index])
        active = (group_index != 0).astype(jnp.float32)
        fields = blend_rows(fields, precursor, first_row, active)
        divergence = centered_x(fields[0]) + centered_y(wrap_y(fields[1])) + centered_z(fields[2])
        pressure = poisson(divergence)
        gradient = jnp.stack([centered_x(pressure), centered_y(wrap_y(pressure)), centered_z(pressure)])
        return fields - gradient

    return lax.map(one_group, jnp.arange(GROUPS, dtype=jnp.int32))
```

```python
import functools
import math

import jax
import jax.numpy as jnp
import ml_dtypes
import numpy as np
from jax import lax
from jax.experimental import pallas as pl
from jax.experimental.pallas import tpu as pltpu
from jax.sharding import PartitionSpec as P

FR = 32
NX = 256
NY = 256
NZ = 128
SLABS = 32
ROWS = 8
EXT = ROWS + 2
CELLS = NX * ROWS
DRAG = 0.5 * 0.75
VMEM_LIMIT = 48 * 2**20


def split_bf16(table):
    high = table.astype(np.float32).astype(ml_dtypes.bfloat16)
    low = (table - high.astype(np.float64)).astype(np.float32).astype(ml_dtypes.bfloat16)
    return high, low


def x_table():
    half = NX // 2
    x = np.arange(NX)
    wave = np.concatenate([np.arange(half + 1), np.arange(1, half)])
    angle = 2.0 * math.pi / NX * ((wave[:, None] * x[None, :]) % NX)
    basis = np.where((np.arange(NX) <= half)[:, None], np.cos(angle), np.sin(angle))
    weight = np.where((wave == 0) | (wave == half), 1.0, 2.0) / NX
    return basis * np.sqrt(weight)[:, None], wave


def z_table():
    m = np.arange(NZ)
    angle = math.pi / (2.0 * NZ) * ((m[:, None] * (2 * m[None, :] + 1)) % (4 * NZ))
    weight = np.where(m == 0, 1.0, 2.0) / NZ
    return np.cos(angle) * np.sqrt(weight)[:, None]


def line_tables():
    wave = x_table()[1]
    minus_x = 4.0 * np.sin(math.pi * wave / NX) ** 2
    minus_z = 4.0 * np.sin(math.pi * np.arange(NZ) / (2.0 * NZ)) ** 2
    total = minus_x[:, None] + minus_z[None, :]
    theta = 2.0 * np.arcsinh(np.sqrt(total) / 2.0)
    zero = total == 0.0
    theta = np.where(zero, 1.0, theta)
    mu = np.exp(-theta)
    scale = -1.0 / (2.0 * np.sinh(theta))
    wrap = 1.0 / (-np.expm1(-NY * theta))
    tables = [mu, np.exp(theta), scale, np.exp(-ROWS * theta), wrap]
    return [np.where(zero, 0.0, t).astype(np.float32) for t in tables]


def dot3(a_high, a_low, b_high, b_low):
    dot = functools.partial(jnp.dot, preferred_element_type=jnp.float32)
    return dot(a_high, b_high) + (dot(a_high, b_low) + dot(a_low, b_high))


def parts(value):
    high = value.astype(jnp.bfloat16)
    low = (value - high.astype(jnp.float32)).astype(jnp.bfloat16)
    return high, low


def call(body, outs, name, scratch=(), in_specs=None, flops=0, nbytes=0, **kw):
    return pl.pallas_call(
        body,
        out_shape=[jax.ShapeDtypeStruct(s, jnp.float32) for s in outs],
        in_specs=in_specs,
        out_specs=[pl.BlockSpec(memory_space=pltpu.VMEM)] * len(outs),
        scratch_shapes=list(scratch),
        compiler_params=pltpu.CompilerParams(vmem_limit_bytes=VMEM_LIMIT),
        cost_estimate=pl.CostEstimate(flops=flops, bytes_accessed=nbytes, transcendentals=0),
        name=name,
        **kw,
    )


VM = pl.BlockSpec(memory_space=pltpu.VMEM)
SM = pl.BlockSpec(memory_space=pltpu.SMEM)


def every8(first, count=NX):
    return pl.ds(first, count, stride=ROWS)


def edges_kernel(start_ref, vel_ref, visc_ref, low_ref, high_ref, fringe_ref):
    for row, out in ((0, low_ref), (ROWS - 1, high_ref)):
        for c in range(3):
            out[c] = vel_ref[c, every8(row), :]
        out[3] = visc_ref[every8(row), :]
    first = pl.multiple_of(start_ref[0] * ROWS, ROWS)
    for c in range(3):
        fringe_ref[pl.ds(c * FR * ROWS, FR * ROWS), :] = vel_ref[c, pl.ds(first, FR * ROWS), :]


def iotas():
    return (
        lax.broadcasted_iota(jnp.int32, (ROWS, NZ), 0),
        lax.broadcasted_iota(jnp.int32, (ROWS, NZ), 1),
    )


def tile(x):
    return pl.ds(pl.multiple_of(x * ROWS, ROWS), ROWS)


def diffuse_kernel(vel_ref, visc_ref, turb_ref, own_low, own_high, prev_ref, next_ref, out_ref, rim):
    del own_low, own_high
    for c in range(4):
        rim[c, every8(0), :] = prev_ref[c]
        rim[c, every8(ROWS - 1), :] = next_ref[c]
    row, lane = iotas()
    first_row, last_row = row == 0, row == ROWS - 1
    first_lane, last_lane = lane == 0, lane == NZ - 1

    def fields_at(x):
        return [vel_ref[c, tile(x), :] for c in range(3)], visc_ref[tile(x), :]

    def flux(nu_sum, a, b):
        return nu_sum * (b - a)

    def step(x, carry):
        now, nu, back = carry
        ahead, nu_ahead = fields_at(lax.rem(x + 1, NX))
        nu_rim = rim[3, tile(x), :]
        half = 0.5 * nu
        sum_x = half + 0.5 * nu_ahead
        half_rim = half + 0.5 * nu_rim
        sum_y = jnp.where(last_row, half_rim, half + pltpu.roll(half, ROWS - 1, 0))
        sum_z = jnp.where(last_lane, 0.0, half + pltpu.roll(half, NZ - 1, 1))
        fluxes = []
        for c in range(3):
            u = now[c]
            edge = rim[c, tile(x), :]
            flux_x = sum_x * (ahead[c] - u)
            flux_y = sum_y * (jnp.where(last_row, edge, pltpu.roll(u, ROWS - 1, 0)) - u)
            down_y = jnp.where(first_row, half_rim * (u - edge), pltpu.roll(flux_y, 1, 0))
            flux_z = sum_z * (pltpu.roll(u, NZ - 1, 1) - u)
            down_z = pltpu.roll(flux_z, 1, 1)
            new = u + (flux_x - back[c]) + (flux_y - down_y) + (flux_z - down_z)
            if c == 0:
                disc = turb_ref[tile(x), :].astype(jnp.float32)
                new = new - DRAG * disc * new * jnp.abs(new)
            out_ref[c, tile(x), :] = new
            fluxes.append(flux_x)
        return ahead, nu_ahead, fluxes

    del first_lane
    last, nu_last = fields_at(NX - 1)
    now, nu = fields_at(0)
    sum_x = 0.5 * nu_last + 0.5 * nu
    back = [flux(sum_x, last[c], now[c]) for c in range(3)]
    lax.fori_loop(0, NX, step, (now, nu, back), unroll=4)


def centred_z(value, first_lane, last_lane):
    up = jnp.where(last_lane, value, pltpu.roll(value, NZ - 1, 1))
    down = jnp.where(first_lane, value, pltpu.roll(value, 1, 1))
    return up - down


def forward_kernel(
    start_ref, field_ref, q0, q1, q2, q3, profile_ref, xh, xl, zh, zl, mu_ref,
    out_ref, hat_ref, pay_ref, rim_ref, fringe, div, modes,
):
    me = lax.axis_index("sim")
    active = jnp.where(me == 0, 0.0, 1.0).astype(jnp.float32)
    quarter = 3 * FR * ROWS // 4
    for k, part in enumerate((q0, q1, q2, q3)):
        at = lax.rem(lax.rem(me, 4) + 4 - k, 4)
        fringe[pl.ds(pl.multiple_of(at * quarter, ROWS), quarter), :] = part[...]
    row, lane = iotas()
    first_row, last_row = row == 0, row == ROWS - 1
    first_lane, last_lane = lane == 0, lane == NZ - 1

    for c in range(3):
        out_ref[c] = field_ref[c]
    start = start_ref[0]

    def blend(i, _):
        weight = profile_ref[i] * active
        for c in range(3):
            old = out_ref[c, tile(start + i), :]
            out_ref[c, tile(start + i), :] = old + weight * (fringe[tile(c * FR + i), :] - old)
        return 0

    lax.fori_loop(0, FR, blend, 0, unroll=4)

    def source(x, carry):
        behind, now = carry
        ahead = out_ref[0, tile(lax.rem(x + 1, NX)), :]
        v = out_ref[1, tile(x), :]
        w = out_ref[2, tile(x), :]
        up = jnp.where(last_row, 0.0, pltpu.roll(v, ROWS - 1, 0))
        down = jnp.where(first_row, 0.0, pltpu.roll(v, 1, 0))
        div[tile(x), :] = 0.5 * ((ahead - behind) + (up - down) + centred_z(w, first_lane, last_lane))
        return now, ahead

    lax.fori_loop(0, NX, source, (out_ref[0, tile(NX - 1), :], out_ref[0, tile(0), :]), unroll=4)

    z_high, z_low = zh[...], zl[...]
    for block in range(8):
        rows = pl.ds(block * NX, NX)
        modes[rows, :] = dot3(*parts(div[rows, :]), z_high, z_low)
    low = out_ref[1, every8(0), :]
    high = out_ref[1, every8(ROWS - 1), :]
    rim_ref[0] = low
    rim_ref[1] = high
    low = dot3(*parts(0.5 * low), z_high, z_low)
    high = dot3(*parts(-0.5 * high), z_high, z_low)
    x_high, x_low = xh[...], xl[...]
    for r in range(0, EXT, 2):
        pair = []
        for k in (r, r + 1):
            pair.append(low if k == 0 else high if k == EXT - 1 else modes[every8(k - 1), :])
        both = dot3(x_high, x_low, *parts(jnp.concatenate(pair, 1)))
        hat_ref[r] = both[:, :NZ]
        hat_ref[r + 1] = both[:, NZ:]

    origin = (row == 0) & (lane == 0)

    def sums(block, at):
        mu = mu_ref[at, :]
        rows = [hat_ref[r, at, :] for r in range(EXT)]
        right = rows[0]
        for value in rows[1:]:
            right = mu * right + value
        left = rows[-1]
        for value in rows[-2::-1]:
            left = mu * left + value
        return right, left, rows

    def weigh(block, _):
        right, left, _ = sums(block, tile(block))
        pay_ref[block, 0] = right
        pay_ref[block, 1] = left
        return 0

    lax.fori_loop(1, NX // ROWS, weigh, 0, unroll=2)
    right, left, rows = sums(0, tile(0))
    moment0 = functools.reduce(jnp.add, rows)
    moment1 = functools.reduce(jnp.add, [float(r - 1) * rows[r] for r in range(EXT) if r != 1])
    pay_ref[0, 0] = jnp.where(origin, moment0, right)
    pay_ref[0, 1] = jnp.where(origin, moment1, left)


def far_kernel(pay_ref, step_ref, wrap_ref, out_ref):
    slab = lax.axis_index("slab")
    step = step_ref[tile(slab), :]
    wrap = wrap_ref[tile(slab), :]
    row, lane = iotas()
    origin = (row == 0) & (lane == 0) & (slab == 0)
    right = jnp.zeros((ROWS, NZ), jnp.float32)
    left = right
    total0 = right
    total1 = right
    ramp = right
    for s in range(SLABS):
        right = step * right + pay_ref[s, 0]
        left = step * left + pay_ref[SLABS - 1 - s, 1]
        total0 = total0 + pay_ref[s, 0]
        total1 = total1 + pay_ref[s, 1]
        ramp = ramp + float((SLABS - s) % SLABS) * pay_ref[s, 0]
    right = right * wrap
    left = left * wrap
    for s in range(SLABS):
        m0, m1 = pay_ref[s, 0], pay_ref[s, 1]
        if s:
            ramp = ramp + total0 - float(SLABS) * m0
        slope = 0.5 * (total0 - m0) - (ROWS / NY) * ramp + (1.0 / NY) * (total1 - m1)
        out_ref[s, 0] = jnp.where(origin, slope, right)
        right = step * right + m0
        t = SLABS - 1 - s
        curve = (-0.5 / NY) * (total0 - pay_ref[t, 0])
        out_ref[t, 1] = jnp.where(origin, curve, left)
        left = step * left + pay_ref[t, 1]


def green0(j):
    return 0.5 * j - j * j / (2.0 * NY)


def final_kernel(
    field_ref, hat_ref, ret_ref, prev_ref, next_ref, xh, xl, zh, zl, mu_ref, inv_ref, scale_ref,
    out_ref, press, field, rim,
):
    row, lane = iotas()
    first_row, last_row = row == 0, row == ROWS - 1
    first_lane, last_lane = lane == 0, lane == NZ - 1
    origin = (row == 0) & (lane == 0)

    def solve(block, at):
        mu, inv, scale = mu_ref[at, :], inv_ref[at, :], scale_ref[at, :]
        rows = [hat_ref[r, at, :] for r in range(EXT)]
        below = [ret_ref[block, 0] * inv + rows[0]]
        for value in rows[1:]:
            below.append(mu * below[-1] + value)
        above = [ret_ref[block, 1] * inv]
        for value in rows[:0:-1]:
            above.append(mu * (above[-1] + value))
        above.reverse()
        return [scale * (a + b) for a, b in zip(below, above)], rows

    def line(block, _):
        at = tile(block)
        values, _ = solve(block, at)
        for r in range(EXT):
            press[r, at, :] = values[r]
        return 0

    lax.fori_loop(1, NX // ROWS, line, 0, unroll=2)
    at = pl.ds(0, ROWS)
    values, rows = solve(0, at)
    slope, curve = ret_ref[0, 0], ret_ref[0, 1]
    for r in range(EXT):
        y = float(r - 1)
        mean_line = slope * y + curve * (y * y)
        for k in range(EXT):
            if k != r:
                mean_line = mean_line + green0(float(abs(r - k))) * rows[k]
        press[r, at, :] = jnp.where(origin, mean_line, values[r])

    x_high, x_low = xh[...], xl[...]
    z_high, z_low = zh[...], zl[...]
    for r in range(0, EXT, 2):
        pair = jnp.concatenate([press[r], press[r + 1]], 1)
        both = dot3(x_high, x_low, *parts(pair))
        for k in (r, r + 1):
            plane = both[:, :NZ] if k == r else both[:, NZ:]
            plane = dot3(*parts(plane), z_high, z_low)
            if k == 0:
                rim[every8(0), :] = plane - 0.5 * prev_ref[...]
            elif k == EXT - 1:
                rim[every8(ROWS - 1), :] = plane + 0.5 * next_ref[...]
            else:
                field[every8(k - 1), :] = plane

    def project(x, carry):
        behind, now = carry
        ahead = field[tile(lax.rem(x + 1, NX)), :]
        edge = rim[tile(x), :]
        up = jnp.where(last_row, edge, pltpu.roll(now, ROWS - 1, 0))
        down = jnp.where(first_row, edge, pltpu.roll(now, 1, 0))
        grads = (ahead - behind, up - down, centred_z(now, first_lane, last_lane))
        for c in range(3):
            out_ref[c, tile(x), :] = field_ref[c, tile(x), :] - 0.5 * grads[c]
        return now, ahead

    lax.fori_loop(0, NX, project, (field[tile(NX - 1), :], field[tile(0), :]), unroll=4)


def fringe_quarters(fringe):
    quarter = fringe.shape[0] // 4
    me = lax.axis_index("sim")
    piece = [fringe[k * quarter : (k + 1) * quarter] for k in range(4)]
    mine = piece[0]
    for k in (1, 2, 3):
        came = lax.ppermute(piece[k], "sim", [(0, k)])
        mine = jnp.where(me == k, came, mine)
    came = lax.ppermute(mine, "sim", [(i, i + 4) for i in range(4)])
    mine = jnp.where(me >= 4, came, mine)
    quarters = [mine]
    for k in (1, 2, 3):
        pairs = [(4 * z + i, 4 * z + (i + k) % 4) for z in range(2) for i in range(4)]
        quarters.append(lax.ppermute(mine, "sim", pairs))
    return quarters


def local(velocity, viscosity, turbines, fringe_start):
    vel = velocity.reshape(3, CELLS, NZ)
    visc = viscosity.reshape(CELLS, NZ)
    turb = turbines.reshape(CELLS, NZ)
    x_basis = x_table()[0]
    z_basis = z_table()
    to_x, from_x = split_bf16(x_basis), split_bf16(x_basis.T)
    to_z, from_z = split_bf16(z_basis.T), split_bf16(z_basis)
    mu, inv, scale, step, wrap = line_tables()
    profile = (np.sin(math.pi * (np.arange(FR) + 0.5) / FR) ** 2).astype(np.float32)
    upward = [(i, (i + 1) % SLABS) for i in range(SLABS)]
    downward = [((i + 1) % SLABS, i) for i in range(SLABS)]

    low, high, fringe = call(
        edges_kernel,
        [(4, NX, NZ), (4, NX, NZ), (3 * FR * ROWS, NZ)],
        "edges",
        in_specs=[SM, VM, VM],
        nbytes=6 * 2**20,
    )(fringe_start, vel, visc)
    prev = lax.ppermute(high, "slab", upward)
    following = lax.ppermute(low, "slab", downward)
    quarters = fringe_quarters(fringe)
    (fields,) = call(
        diffuse_kernel,
        [(3, CELLS, NZ)],
        "diffuse",
        in_specs=[VM] * 7,
        scratch=[pltpu.VMEM((4, CELLS, NZ), jnp.float32)],
        flops=2**26,
        nbytes=12 * 2**20,
    )(vel, visc, turb, low, high, prev, following)
    fields, hat, pay, rims = call(
        forward_kernel,
        [(3, CELLS, NZ), (EXT, NX, NZ), (SLABS, 2, ROWS, NZ), (2, NX, NZ)],
        "forward",
        in_specs=[SM] + [VM] * 5 + [SM] + [VM] * 5,
        scratch=[
            pltpu.VMEM((3 * FR * ROWS, NZ), jnp.float32),
            pltpu.VMEM((CELLS, NZ), jnp.float32),
            pltpu.VMEM((CELLS, NZ), jnp.float32),
        ],
        flops=2**30,
        nbytes=10 * 2**20,
    )(fringe_start, fields, *quarters, profile, *to_x, *to_z, mu)
    v_prev = lax.ppermute(rims[1], "slab", upward)
    v_next = lax.ppermute(rims[0], "slab", downward)
    pay = lax.all_to_all(pay, "slab", split_axis=0, concat_axis=0, tiled=True)
    (ret,) = call(
        far_kernel,
        [(SLABS, 2, ROWS, NZ)],
        "far",
        in_specs=[VM] * 3,
        nbytes=2**19,
    )(pay, step, wrap)
    ret = lax.all_to_all(ret, "slab", split_axis=0, concat_axis=0, tiled=True)
    (out,) = call(
        final_kernel,
        [(3, CELLS, NZ)],
        "final",
        in_specs=[VM] * 12,
        scratch=[
            pltpu.VMEM((EXT, NX, NZ), jnp.float32),
            pltpu.VMEM((CELLS, NZ), jnp.float32),
            pltpu.VMEM((CELLS, NZ), jnp.float32),
        ],
        flops=2**30,
        nbytes=10 * 2**20,
    )(fields, hat, ret, v_prev, v_next, *from_x, *from_z, mu, inv, scale)
    return out.reshape(velocity.shape)


def solution(mesh):
    return jax.shard_map(
        local,
        mesh=mesh,
        in_specs=(
            P("sim", None, None, "slab", None),
            P("sim", None, "slab", None),
            P("sim", None, "slab", None),
            P(),
        ),
        out_specs=P("sim", None, None, "slab", None),
        check_vma=False,
    )
```

```python
import functools
import math

import jax
import jax.numpy as jnp
import numpy as np
from jax import lax
from jax.experimental import pallas as pl
from jax.experimental.pallas import tpu as pltpu
from jax.sharding import PartitionSpec as P

FR = 32
NX = 256
NY = 256
NZ = 128
SLABS = 32
ROWS = 8
EXT = ROWS + 2
CELLS = NX * ROWS
DRAG = 0.5 * 0.75
MIB = 2**20
DIFFUSE_ROOM = 40
FORWARD_ROOM = 40


def x_table():
    half = NX // 2
    x = np.arange(NX)
    wave = np.concatenate([np.arange(half + 1), np.arange(1, half)])
    angle = 2.0 * math.pi / NX * ((wave[:, None] * x[None, :]) % NX)
    basis = np.where((np.arange(NX) <= half)[:, None], np.cos(angle), np.sin(angle))
    weight = np.where((wave == 0) | (wave == half), 1.0, 2.0) / NX
    return basis * np.sqrt(weight)[:, None], wave


def z_table():
    m = np.arange(NZ)
    angle = math.pi / (2.0 * NZ) * ((m[:, None] * (2 * m[None, :] + 1)) % (4 * NZ))
    weight = np.where(m == 0, 1.0, 2.0) / NZ
    return np.cos(angle) * np.sqrt(weight)[:, None]


def line_tables():
    wave = x_table()[1]
    minus_x = 4.0 * np.sin(math.pi * wave / NX) ** 2
    minus_z = 4.0 * np.sin(math.pi * np.arange(NZ) / (2.0 * NZ)) ** 2
    total = minus_x[:, None] + minus_z[None, :]
    theta = 2.0 * np.arcsinh(np.sqrt(total) / 2.0)
    zero = total == 0.0
    theta = np.where(zero, 1.0, theta)
    mu = np.exp(-theta)
    wrap = 1.0 / (-np.expm1(-NY * theta))
    tables = [mu, np.exp(-ROWS * theta), wrap]
    return [np.where(zero, 0.0, t).astype(np.float32) for t in tables]


def dot3(a_high, a_low, b_high, b_low):
    dot = functools.partial(jnp.dot, preferred_element_type=jnp.float32)
    return dot(a_high, b_high) + (dot(a_high, b_low) + dot(a_low, b_high))


def parts(value):
    high = value.astype(jnp.bfloat16)
    low = (value - high.astype(jnp.float32)).astype(jnp.bfloat16)
    return high, low


def call(body, outs, name, scratch=(), in_specs=None, out_specs=None, room=20, flops=0, nbytes=0, **kw):
    return pl.pallas_call(
        body,
        out_shape=[jax.ShapeDtypeStruct(s, jnp.float32) for s in outs],
        in_specs=in_specs,
        out_specs=out_specs or [VM] * len(outs),
        scratch_shapes=list(scratch),
        compiler_params=pltpu.CompilerParams(vmem_limit_bytes=room * MIB),
        cost_estimate=pl.CostEstimate(flops=flops, bytes_accessed=nbytes, transcendentals=0),
        name=name,
        **kw,
    )


VM = pl.BlockSpec(memory_space=pltpu.VMEM)
SM = pl.BlockSpec(memory_space=pltpu.SMEM)
HB = pl.BlockSpec(memory_space=pltpu.HBM)


def start_all(pairs, sems):
    copies = [pltpu.make_async_copy(a, b, sems.at[k]) for k, (a, b) in enumerate(pairs)]
    for copy in copies:
        copy.start()
    return copies


def wait_all(copies):
    for copy in copies:
        copy.wait()


def every8(first, count=NX):
    return pl.ds(first, count, stride=ROWS)


def fringe_kernel(start_ref, vel_ref, q0, q1, q2, q3, sems):
    first = pl.multiple_of(start_ref[0] * ROWS, ROWS)
    rows = FR * ROWS
    quarter = 3 * rows // 4
    pairs = []
    for k, out in enumerate((q0, q1, q2, q3)):
        at = k * quarter
        while at < (k + 1) * quarter:
            c, inner = divmod(at, rows)
            size = min(rows - inner, (k + 1) * quarter - at)
            pairs.append((vel_ref.at[c, pl.ds(first + inner, size)], out.at[pl.ds(at - k * quarter, size)]))
            at += size
    wait_all(start_all(pairs, sems))


EDGE_CHUNKS = 4


def edges_kernel(vel_in, visc_in, low_ref, high_ref, vel_ref, visc_ref, sems):
    part = CELLS // EDGE_CHUNKS
    pairs = []
    for k in range(EDGE_CHUNKS):
        rows = pl.ds(k * part, part)
        pairs += [(vel_in.at[c, rows], vel_ref.at[c, rows]) for c in range(3)]
        pairs.append((visc_in.at[rows], visc_ref.at[rows]))
    copies = start_all(pairs, sems)
    count = NX // EDGE_CHUNKS
    for k in range(EDGE_CHUNKS):
        wait_all(copies[4 * k : 4 * k + 4])
        for row, out in ((0, low_ref), (ROWS - 1, high_ref)):
            for c in range(3):
                out[c, pl.ds(k * count, count), :] = vel_ref[c, every8(k * part + row, count), :]
            out[3, pl.ds(k * count, count), :] = visc_ref[every8(k * part + row, count), :]


def iotas():
    return (
        lax.broadcasted_iota(jnp.int32, (ROWS, NZ), 0),
        lax.broadcasted_iota(jnp.int32, (ROWS, NZ), 1),
    )


def tile(x):
    return pl.ds(pl.multiple_of(x * ROWS, ROWS), ROWS)


CHUNKS = 8


def diffuse_kernel(vel_in, visc_in, turb_in, prev_in, next_in, out_ref, vel_ref, visc_ref, turb_ref, prev_ref, next_ref, rim, sems):
    part = CELLS // CHUNKS
    spans = [pl.ds(k * part, part) for k in (CHUNKS - 1, *range(CHUNKS - 1))]
    pairs = [(prev_in, prev_ref), (next_in, next_ref)]
    for span in spans:
        pairs += [(vel_in.at[:, span], vel_ref.at[:, span]), (visc_in.at[span], visc_ref.at[span])]
        pairs.append((turb_in.at[span], turb_ref.at[span]))
    copies = start_all(pairs, sems)
    wait_all(copies[:2])
    for c in range(4):
        rim[c, every8(0), :] = prev_ref[c]
        rim[c, every8(ROWS - 1), :] = next_ref[c]
    wait_all(copies[2:8])
    row, lane = iotas()
    first_row, last_row = row == 0, row == ROWS - 1
    first_lane, last_lane = lane == 0, lane == NZ - 1

    def fields_at(x):
        return [vel_ref[c, tile(x), :] for c in range(3)], visc_ref[tile(x), :]

    def flux(nu_sum, a, b):
        return nu_sum * (b - a)

    def step(x, carry):
        now, nu, back = carry
        ahead, nu_ahead = fields_at(lax.rem(x + 1, NX))
        nu_rim = rim[3, tile(x), :]
        half = 0.5 * nu
        sum_x = half + 0.5 * nu_ahead
        half_rim = half + 0.5 * nu_rim
        sum_y = jnp.where(last_row, half_rim, half + pltpu.roll(half, ROWS - 1, 0))
        sum_z = jnp.where(last_lane, 0.0, half + pltpu.roll(half, NZ - 1, 1))
        fluxes = []
        for c in range(3):
            u = now[c]
            edge = rim[c, tile(x), :]
            flux_x = sum_x * (ahead[c] - u)
            flux_y = sum_y * (jnp.where(last_row, edge, pltpu.roll(u, ROWS - 1, 0)) - u)
            down_y = jnp.where(first_row, half_rim * (u - edge), pltpu.roll(flux_y, 1, 0))
            flux_z = sum_z * (pltpu.roll(u, NZ - 1, 1) - u)
            down_z = pltpu.roll(flux_z, 1, 1)
            new = u + (flux_x - back[c]) + (flux_y - down_y) + (flux_z - down_z)
            if c == 0:
                disc = turb_ref[tile(x), :].astype(jnp.float32)
                new = new - DRAG * disc * new * jnp.abs(new)
            out_ref[c, tile(x), :] = new
            fluxes.append(flux_x)
        return ahead, nu_ahead, fluxes

    del first_lane
    last, nu_last = fields_at(NX - 1)
    now, nu = fields_at(0)
    sum_x = 0.5 * nu_last + 0.5 * nu
    back = [flux(sum_x, last[c], now[c]) for c in range(3)]
    carry = (now, nu, back)
    count = NX // CHUNKS
    for k in range(CHUNKS):
        if k < CHUNKS - 2:
            wait_all(copies[8 + 3 * k : 11 + 3 * k])
        carry = lax.fori_loop(k * count, (k + 1) * count, step, carry, unroll=16)


def centred_z(value, first_lane, last_lane):
    up = jnp.where(last_lane, value, pltpu.roll(value, NZ - 1, 1))
    down = jnp.where(first_lane, value, pltpu.roll(value, 1, 1))
    return up - down


TAB_X = NX
TAB_Z = TAB_X + 2 * NX
LATER = TAB_Z + NZ
STORE_HAT = 3 * CELLS
STORE_LATER = STORE_HAT + EXT * NX
STORE = 40 * 2**11


def x_matrix(table_ref):
    return jnp.concatenate([table_ref[pl.ds(TAB_X, NX), :], table_ref[pl.ds(TAB_X + NX, NX), :]], 1)


def forward_kernel(
    start_ref, field_ref, q0, q1, q2, q3, profile_ref, table_ref, later_ref,
    store, pay_ref, low_ref, high_ref, out_ref, fringe, div, modes, hat_ref, sems,
):
    copies = start_all([(later_ref, store.at[pl.ds(STORE_LATER, LATER)])], sems)
    me = lax.axis_index("sim")
    active = jnp.where(me == 0, 0.0, 1.0).astype(jnp.float32)
    quarter = 3 * FR * ROWS // 4
    for k, part in enumerate((q0, q1, q2, q3)):
        at = lax.rem(lax.rem(me, 4) + 4 - k, 4)
        fringe[pl.ds(pl.multiple_of(at * quarter, ROWS), quarter), :] = part[...]
    row, lane = iotas()
    first_row, last_row = row == 0, row == ROWS - 1
    first_lane, last_lane = lane == 0, lane == NZ - 1

    for c in range(3):
        out_ref[c] = field_ref[c]
    start = start_ref[0]

    def blend(i, _):
        weight = profile_ref[i] * active
        for c in range(3):
            old = out_ref[c, tile(start + i), :]
            out_ref[c, tile(start + i), :] = old + weight * (fringe[tile(c * FR + i), :] - old)
        return 0

    lax.fori_loop(0, FR, blend, 0, unroll=8)
    for c in range(3):
        copies.append(pltpu.make_async_copy(out_ref.at[c], store.at[pl.ds(c * CELLS, CELLS)], sems.at[1 + c]))
        copies[-1].start()

    def source(x, carry):
        behind, now = carry
        ahead = out_ref[0, tile(lax.rem(x + 1, NX)), :]
        v = out_ref[1, tile(x), :]
        w = out_ref[2, tile(x), :]
        up = jnp.where(last_row, 0.0, pltpu.roll(v, ROWS - 1, 0))
        down = jnp.where(first_row, 0.0, pltpu.roll(v, 1, 0))
        div[tile(x), :] = 0.5 * ((ahead - behind) + (up - down) + centred_z(w, first_lane, last_lane))
        return now, ahead

    lax.fori_loop(0, NX, source, (out_ref[0, tile(NX - 1), :], out_ref[0, tile(0), :]), unroll=16)

    z_high, z_low = parts(table_ref[pl.ds(TAB_Z, NZ), :])
    for block in range(8):
        rows = pl.ds(block * NX, NX)
        modes[rows, :] = dot3(*parts(div[rows, :]), z_high, z_low)
    low = out_ref[1, every8(0), :]
    high = out_ref[1, every8(ROWS - 1), :]
    low_ref[...] = low
    high_ref[...] = high
    low = dot3(*parts(0.5 * low), z_high, z_low)
    high = dot3(*parts(-0.5 * high), z_high, z_low)
    x_high, x_low = parts(x_matrix(table_ref))
    for r in range(0, EXT, 2):
        pair = []
        for k in (r, r + 1):
            pair.append(low if k == 0 else high if k == EXT - 1 else modes[every8(k - 1), :])
        both = dot3(x_high, x_low, *parts(jnp.concatenate(pair, 1)))
        hat_ref[r] = both[:, :NZ]
        hat_ref[r + 1] = both[:, NZ:]
        for k in (r, r + 1):
            to = store.at[pl.ds(STORE_HAT + k * NX, NX)]
            copies.append(pltpu.make_async_copy(hat_ref.at[k], to, sems.at[4 + k]))
            copies[-1].start()

    origin = (row == 0) & (lane == 0)

    def sums(block, at):
        mu = table_ref[at, :]
        rows = [hat_ref[r, at, :] for r in range(EXT)]
        right = rows[0]
        for value in rows[1:]:
            right = mu * right + value
        left = rows[-1]
        for value in rows[-2::-1]:
            left = mu * left + value
        return right, left, rows

    def weigh(block, _):
        right, left, _ = sums(block, tile(block))
        pay_ref[block, 0] = right
        pay_ref[block, 1] = left
        return 0

    lax.fori_loop(1, NX // ROWS, weigh, 0, unroll=4)
    right, left, rows = sums(0, tile(0))
    moment0 = functools.reduce(jnp.add, rows)
    moment1 = functools.reduce(jnp.add, [float(r - 1) * rows[r] for r in range(EXT) if r != 1])
    pay_ref[0, 0] = jnp.where(origin, moment0, right)
    pay_ref[0, 1] = jnp.where(origin, moment1, left)
    wait_all(copies)


def far_kernel(pay_ref, step_ref, wrap_ref, out_ref):
    slab = lax.axis_index("slab")
    step = step_ref[tile(slab), :]
    wrap = wrap_ref[tile(slab), :]
    row, lane = iotas()
    origin = (row == 0) & (lane == 0) & (slab == 0)
    right = jnp.zeros((ROWS, NZ), jnp.float32)
    left = right
    total0 = right
    total1 = right
    ramp = right
    for s in range(SLABS):
        right = step * right + pay_ref[s, 0]
        left = step * left + pay_ref[SLABS - 1 - s, 1]
        total0 = total0 + pay_ref[s, 0]
        total1 = total1 + pay_ref[s, 1]
        ramp = ramp + float((SLABS - s) % SLABS) * pay_ref[s, 0]
    right = right * wrap
    left = left * wrap
    for s in range(SLABS):
        m0, m1 = pay_ref[s, 0], pay_ref[s, 1]
        if s:
            ramp = ramp + total0 - float(SLABS) * m0
        slope = 0.5 * (total0 - m0) - (ROWS / NY) * ramp + (1.0 / NY) * (total1 - m1)
        out_ref[s, 0] = jnp.where(origin, slope, right)
        right = step * right + m0
        t = SLABS - 1 - s
        curve = (-0.5 / NY) * (total0 - pay_ref[t, 0])
        out_ref[t, 1] = jnp.where(origin, curve, left)
        left = step * left + pay_ref[t, 1]


OUT_CHUNKS = 4


def green0(j):
    return 0.5 * j - j * j / (2.0 * NY)


def final_kernel(
    ret_ref, prev_ref, next_ref, store,
    out_hbm, press, field, rim, out_ref, field_ref, hat_ref, table_ref, sems, out_sems,
):
    hats = [(store.at[pl.ds(STORE_HAT + r * NX, NX)], hat_ref.at[r]) for r in range(EXT)]
    lines = (pl.ds(0, NX), pl.ds(NX, LATER - NX))
    later = [(store.at[pl.ds(STORE_LATER + s.start, s.size)], table_ref.at[s]) for s in lines]
    fields = [(store.at[pl.ds(c * CELLS, CELLS)], field_ref.at[c]) for c in range(3)]
    copies = start_all([later[0], *hats, later[1], *fields], sems)
    wait_all(copies[: 1 + EXT])
    row, lane = iotas()
    first_row, last_row = row == 0, row == ROWS - 1
    first_lane, last_lane = lane == 0, lane == NZ - 1
    origin = (row == 0) & (lane == 0)

    def solve(block, at):
        mu = table_ref[at, :]
        inv = 1.0 / jnp.where(mu == 0.0, 1.0, mu)
        scale = jnp.where(mu == 0.0, 0.0, -1.0 / ((1.0 + mu) * (1.0 - mu) * inv))
        rows = [hat_ref[r, at, :] for r in range(EXT)]
        below = [ret_ref[block, 0] * inv + rows[0]]
        for value in rows[1:]:
            below.append(mu * below[-1] + value)
        above = [ret_ref[block, 1] * inv]
        for value in rows[:0:-1]:
            above.append(mu * (above[-1] + value))
        above.reverse()
        return [scale * (a + b) for a, b in zip(below, above)], rows

    def line(block, _):
        at = tile(block)
        values, _ = solve(block, at)
        for r in range(EXT):
            press[r, at, :] = values[r]
        return 0

    lax.fori_loop(1, NX // ROWS, line, 0, unroll=4)
    at = pl.ds(0, ROWS)
    values, rows = solve(0, at)
    slope, curve = ret_ref[0, 0], ret_ref[0, 1]
    for r in range(EXT):
        y = float(r - 1)
        mean_line = slope * y + curve * (y * y)
        for k in range(EXT):
            if k != r:
                mean_line = mean_line + green0(float(abs(r - k))) * rows[k]
        press[r, at, :] = jnp.where(origin, mean_line, values[r])

    copies[1 + EXT].wait()
    x_high, x_low = parts(x_matrix(table_ref))
    z_high, z_low = parts(table_ref[pl.ds(TAB_Z, NZ), :])
    for r in range(0, EXT, 2):
        pair = jnp.concatenate([press[r], press[r + 1]], 1)
        both = dot3(x_high, x_low, *parts(pair))
        for k in (r, r + 1):
            plane = both[:, :NZ] if k == r else both[:, NZ:]
            plane = dot3(*parts(plane), z_high, z_low)
            if k == 0:
                rim[every8(0), :] = plane - 0.5 * prev_ref[...]
            elif k == EXT - 1:
                rim[every8(ROWS - 1), :] = plane + 0.5 * next_ref[...]
            else:
                field[every8(k - 1), :] = plane

    def project(x, carry):
        behind, now = carry
        ahead = field[tile(lax.rem(x + 1, NX)), :]
        edge = rim[tile(x), :]
        up = jnp.where(last_row, edge, pltpu.roll(now, ROWS - 1, 0))
        down = jnp.where(first_row, edge, pltpu.roll(now, 1, 0))
        grads = (ahead - behind, up - down, centred_z(now, first_lane, last_lane))
        for c in range(3):
            out_ref[c, tile(x), :] = field_ref[c, tile(x), :] - 0.5 * grads[c]
        return now, ahead

    carry = (field[tile(NX - 1), :], field[tile(0), :])
    wait_all(copies[2 + EXT :])
    copies = []
    part = CELLS // OUT_CHUNKS
    count = NX // OUT_CHUNKS
    for k in range(OUT_CHUNKS):
        carry = lax.fori_loop(k * count, (k + 1) * count, project, carry, unroll=16)
        rows = pl.ds(k * part, part)
        copies.append(pltpu.make_async_copy(out_ref.at[:, rows], out_hbm.at[:, rows], out_sems.at[k]))
        copies[-1].start()
    wait_all(copies)


def fringe_quarters(piece):
    me = lax.axis_index("sim")
    mine = piece[0]
    for k in (1, 2, 3):
        came = lax.ppermute(piece[k], "sim", [(0, k)])
        mine = jnp.where(me == k, came, mine)
    came = lax.ppermute(mine, "sim", [(i, i + 4) for i in range(4)])
    mine = jnp.where(me >= 4, came, mine)
    quarters = [mine]
    for k in (1, 2, 3):
        pairs = [(4 * z + i, 4 * z + (i + k) % 4) for z in range(2) for i in range(4)]
        quarters.append(lax.ppermute(mine, "sim", pairs))
    return quarters


def local(velocity, viscosity, turbines, fringe_start):
    vel = velocity.reshape(3, CELLS, NZ)
    visc = viscosity.reshape(CELLS, NZ)
    turb = turbines.reshape(CELLS, NZ)
    x_basis = x_table()[0]
    z_basis = z_table()
    mu, step, wrap = line_tables()
    table, later = (
        np.concatenate([mu, x[:, :NZ], x[:, NZ:], z]).astype(np.float32)
        for x, z in ((x_basis, z_basis.T), (x_basis.T, z_basis))
    )
    profile = (np.sin(math.pi * (np.arange(FR) + 0.5) / FR) ** 2).astype(np.float32)
    upward = [(i, (i + 1) % SLABS) for i in range(SLABS)]
    downward = [((i + 1) % SLABS, i) for i in range(SLABS)]

    f32 = jnp.float32
    quarter = (3 * FR * ROWS // 4, NZ)
    plane = (NX, NZ)
    pieces = call(
        fringe_kernel,
        [quarter] * 4,
        "fringe",
        room=60,
        in_specs=[SM, HB],
        scratch=[pltpu.SemaphoreType.DMA((6,))],
        nbytes=2**19,
    )(fringe_start, vel)
    quarters = fringe_quarters(pieces)
    low, high = call(
        edges_kernel,
        [(4, NX, NZ), (4, NX, NZ)],
        "edges",
        room=60,
        in_specs=[HB, HB],
        scratch=[
            pltpu.VMEM((3, CELLS, NZ), f32),
            pltpu.VMEM((CELLS, NZ), f32),
            pltpu.SemaphoreType.DMA((4 * EDGE_CHUNKS,)),
        ],
        nbytes=6 * 2**20,
    )(vel, visc)
    prev = lax.ppermute(high, "slab", upward)
    following = lax.ppermute(low, "slab", downward)
    (fields,) = call(
        diffuse_kernel,
        [(3, CELLS, NZ)],
        "diffuse",
        room=DIFFUSE_ROOM,
        in_specs=[HB] * 5,
        scratch=[
            pltpu.VMEM((3, CELLS, NZ), f32),
            pltpu.VMEM((CELLS, NZ), f32),
            pltpu.VMEM((CELLS, NZ), jnp.int32),
            pltpu.VMEM((4, NX, NZ), f32),
            pltpu.VMEM((4, NX, NZ), f32),
            pltpu.VMEM((4, CELLS, NZ), f32),
            pltpu.SemaphoreType.DMA((2 + 3 * CHUNKS,)),
        ],
        flops=2**26,
        nbytes=12 * 2**20,
    )(vel, visc, turb, prev, following)
    store, pay, v_low, v_high = call(
        forward_kernel,
        [(STORE, NZ), (SLABS, 2, ROWS, NZ), plane, plane],
        "forward",
        room=FORWARD_ROOM,
        in_specs=[SM] + [VM] * 5 + [SM] + [VM] * 2,
        out_specs=[HB, VM, VM, VM],
        scratch=[
            pltpu.VMEM((3, CELLS, NZ), f32),
            pltpu.VMEM((3 * FR * ROWS, NZ), f32),
            pltpu.VMEM((CELLS, NZ), f32),
            pltpu.VMEM((CELLS, NZ), f32),
            pltpu.VMEM((EXT, NX, NZ), f32),
            pltpu.SemaphoreType.DMA((4 + EXT,)),
        ],
        flops=2**30,
        nbytes=10 * 2**20,
    )(fringe_start, fields, *quarters, profile, table, later)
    v_prev = lax.ppermute(v_high, "slab", upward)
    v_next = lax.ppermute(v_low, "slab", downward)
    pay = lax.all_to_all(pay, "slab", split_axis=0, concat_axis=0, tiled=True)
    (ret,) = call(
        far_kernel,
        [(SLABS, 2, ROWS, NZ)],
        "far",
        in_specs=[VM] * 3,
        nbytes=2**19,
    )(pay, step, wrap)
    ret = lax.all_to_all(ret, "slab", split_axis=0, concat_axis=0, tiled=True)
    (out,) = call(
        final_kernel,
        [(3, CELLS, NZ)],
        "final",
        room=FORWARD_ROOM,
        in_specs=[VM, VM, VM, HB],
        out_specs=[HB],
        scratch=[
            pltpu.VMEM((EXT, NX, NZ), f32),
            pltpu.VMEM((CELLS, NZ), f32),
            pltpu.VMEM((CELLS, NZ), f32),
            pltpu.VMEM((3, CELLS, NZ), f32),
            pltpu.VMEM((3, CELLS, NZ), f32),
            pltpu.VMEM((EXT, NX, NZ), f32),
            pltpu.VMEM((LATER, NZ), f32),
            pltpu.SemaphoreType.DMA((5 + EXT,)),
            pltpu.SemaphoreType.DMA((OUT_CHUNKS,)),
        ],
        flops=2**30,
        nbytes=10 * 2**20,
    )(ret, v_prev, v_next, store)
    return out.reshape(velocity.shape)


def solution(mesh):
    return jax.shard_map(
        local,
        mesh=mesh,
        in_specs=(
            P("sim", None, None, "slab", None),
            P("sim", None, "slab", None),
            P("sim", None, "slab", None),
            P(),
        ),
        out_specs=P("sim", None, None, "slab", None),
        check_vma=False,
    )
```

```python
import functools
import math

import jax
import jax.numpy as jnp
import numpy as np
from jax import lax
from jax.experimental import pallas as pl
from jax.experimental.pallas import tpu as pltpu
from jax.sharding import PartitionSpec as P

FR = 32
NX = 256
NY = 256
NZ = 128
SLABS = 32
ROWS = 8
EXT = ROWS + 2
CELLS = NX * ROWS
DRAG = 0.5 * 0.75
MIB = 2**20
DIFFUSE_ROOM = 40
FORWARD_ROOM = 40


def x_table():
    half = NX // 2
    x = np.arange(NX)
    wave = np.concatenate([np.arange(half + 1), np.arange(1, half)])
    angle = 2.0 * math.pi / NX * ((wave[:, None] * x[None, :]) % NX)
    basis = np.where((np.arange(NX) <= half)[:, None], np.cos(angle), np.sin(angle))
    weight = np.where((wave == 0) | (wave == half), 1.0, 2.0) / NX
    return basis * np.sqrt(weight)[:, None], wave


def z_table():
    m = np.arange(NZ)
    angle = math.pi / (2.0 * NZ) * ((m[:, None] * (2 * m[None, :] + 1)) % (4 * NZ))
    weight = np.where(m == 0, 1.0, 2.0) / NZ
    return np.cos(angle) * np.sqrt(weight)[:, None]


def line_tables():
    wave = x_table()[1]
    minus_x = 4.0 * np.sin(math.pi * wave / NX) ** 2
    minus_z = 4.0 * np.sin(math.pi * np.arange(NZ) / (2.0 * NZ)) ** 2
    total = minus_x[:, None] + minus_z[None, :]
    theta = 2.0 * np.arcsinh(np.sqrt(total) / 2.0)
    zero = total == 0.0
    theta = np.where(zero, 1.0, theta)
    mu = np.exp(-theta)
    wrap = 1.0 / (-np.expm1(-NY * theta))
    tables = [mu, np.exp(-ROWS * theta), wrap]
    return [np.where(zero, 0.0, t).astype(np.float32) for t in tables]


def dot3(a_high, a_low, b_high, b_low):
    dot = functools.partial(jnp.dot, preferred_element_type=jnp.float32)
    return dot(a_high, b_high) + (dot(a_high, b_low) + dot(a_low, b_high))


def parts(value):
    high = value.astype(jnp.bfloat16)
    low = (value - high.astype(jnp.float32)).astype(jnp.bfloat16)
    return high, low


def call(body, outs, name, scratch=(), in_specs=None, out_specs=None, room=20, flops=0, nbytes=0, **kw):
    return pl.pallas_call(
        body,
        out_shape=[jax.ShapeDtypeStruct(s, jnp.float32) for s in outs],
        in_specs=in_specs,
        out_specs=out_specs or [VM] * len(outs),
        scratch_shapes=list(scratch),
        compiler_params=pltpu.CompilerParams(vmem_limit_bytes=room * MIB),
        cost_estimate=pl.CostEstimate(flops=flops, bytes_accessed=nbytes, transcendentals=0),
        name=name,
        **kw,
    )


VM = pl.BlockSpec(memory_space=pltpu.VMEM)
SM = pl.BlockSpec(memory_space=pltpu.SMEM)
HB = pl.BlockSpec(memory_space=pltpu.HBM)


def start_all(pairs, sems):
    copies = [pltpu.make_async_copy(a, b, sems.at[k]) for k, (a, b) in enumerate(pairs)]
    for copy in copies:
        copy.start()
    return copies


def wait_all(copies):
    for copy in copies:
        copy.wait()


def every8(first, count=NX):
    return pl.ds(first, count, stride=ROWS)


EDGE_CHUNKS = 4


def edges_kernel(
    start_ref, vel_in, visc_in, q0, q1, q2, q3, low_out, high_out,
    vel_ref, visc_ref, low_ref, high_ref, sems, out_sems, piece_sems,
):
    part = CELLS // EDGE_CHUNKS
    pairs = []
    for k in range(EDGE_CHUNKS):
        rows = pl.ds(k * part, part)
        pairs += [(vel_in.at[:, rows], vel_ref.at[:, rows]), (visc_in.at[rows], visc_ref.at[rows])]
    copies = start_all(pairs, sems)
    count = NX // EDGE_CHUNKS
    outs = []
    for k in range(EDGE_CHUNKS):
        wait_all(copies[2 * k : 2 * k + 2])
        planes = pl.ds(k * count, count)
        for row, out in ((0, low_ref), (ROWS - 1, high_ref)):
            for c in range(3):
                out[c, planes, :] = vel_ref[c, every8(k * part + row, count), :]
            out[3, planes, :] = visc_ref[every8(k * part + row, count), :]
        if k == EDGE_CHUNKS - 1:
            first = pl.multiple_of(start_ref[0] * ROWS, ROWS)
            rows = FR * ROWS
            quarter = 3 * rows // 4
            pairs = []
            for n, out in enumerate((q0, q1, q2, q3)):
                at = n * quarter
                while at < (n + 1) * quarter:
                    c, inner = divmod(at, rows)
                    size = min(rows - inner, (n + 1) * quarter - at)
                    from_rows, to_rows = pl.ds(first + inner, size), pl.ds(at - n * quarter, size)
                    pairs.append((vel_ref.at[c, from_rows], out.at[to_rows]))
                    at += size
            outs += start_all(pairs, piece_sems)
        for side, (plane, to) in enumerate(((low_ref, low_out), (high_ref, high_out))):
            outs.append(pltpu.make_async_copy(plane.at[:, planes], to.at[:, planes], out_sems.at[2 * k + side]))
            outs[-1].start()
    wait_all(outs)


def iotas():
    return (
        lax.broadcasted_iota(jnp.int32, (ROWS, NZ), 0),
        lax.broadcasted_iota(jnp.int32, (ROWS, NZ), 1),
    )


def tile(x):
    return pl.ds(pl.multiple_of(x * ROWS, ROWS), ROWS)


def diffuse_kernel(vel_ref, visc_ref, turb_ref, *refs):
    *_, out_ref, disc_ref = refs
    row, lane = iotas()
    last_row, last_lane = row == ROWS - 1, lane == NZ - 1
    inner = jnp.where((row == 0) | last_row, 0.0, DRAG).astype(jnp.float32)

    def fields_at(x):
        return [vel_ref[c, tile(x), :] for c in range(3)], visc_ref[tile(x), :]

    def step(x, carry):
        now, nu, back = carry
        ahead, nu_ahead = fields_at(lax.rem(x + 1, NX))
        half = 0.5 * nu
        sum_x = half + 0.5 * nu_ahead
        sum_y = jnp.where(last_row, 0.0, half + pltpu.roll(half, ROWS - 1, 0))
        sum_z = jnp.where(last_lane, 0.0, half + pltpu.roll(half, NZ - 1, 1))
        fluxes = []
        for c in range(3):
            u = now[c]
            flux_x = sum_x * (ahead[c] - u)
            flux_y = sum_y * (pltpu.roll(u, ROWS - 1, 0) - u)
            flux_z = sum_z * (pltpu.roll(u, NZ - 1, 1) - u)
            down_y, down_z = pltpu.roll(flux_y, 1, 0), pltpu.roll(flux_z, 1, 1)
            new = u + (flux_x - back[c]) + (flux_y - down_y) + (flux_z - down_z)
            if c == 0:
                disc = turb_ref[tile(x), :].astype(jnp.float32)
                new = new - inner * disc * new * jnp.abs(new)
            out_ref[c, tile(x), :] = new
            fluxes.append(flux_x)
        return ahead, nu_ahead, fluxes

    before, nu_before = fields_at(NX - 1)
    now, nu = fields_at(0)
    sum_x = 0.5 * nu_before + 0.5 * nu
    back = [sum_x * (now[c] - before[c]) for c in range(3)]
    lax.fori_loop(0, NX, step, (now, nu, back), unroll=16)
    for side, at in enumerate((0, ROWS - 1)):
        disc_ref[side] = turb_ref[every8(at), :].astype(jnp.float32)


def centred_z(value, first_lane, last_lane):
    up = jnp.where(last_lane, value, pltpu.roll(value, NZ - 1, 1))
    down = jnp.where(first_lane, value, pltpu.roll(value, 1, 1))
    return up - down


TAB_X = NX
TAB_Z = TAB_X + 2 * NX
LATER = TAB_Z + NZ
STORE_HAT = 3 * CELLS
STORE_LATER = STORE_HAT + EXT * NX
STORE = 40 * 2**11


def x_matrix(table_ref):
    return jnp.concatenate([table_ref[pl.ds(TAB_X, NX), :], table_ref[pl.ds(TAB_X + NX, NX), :]], 1)


def forward_kernel(
    start_ref, field_ref, disc_ref, low_in, high_in, prev_in, next_in, q0, q1, q2, q3, profile_ref, table_ref, later_ref,
    store, pay_ref, low_ref, high_ref, out_ref, rims, fringe, div, modes, hat_ref, sems, rim_sems,
):
    del field_ref
    planes = start_all([(p, rims.at[k]) for k, p in enumerate((low_in, prev_in, high_in, next_in))], rim_sems)
    copies = start_all([(later_ref, store.at[pl.ds(STORE_LATER, LATER)])], sems)
    me = lax.axis_index("sim")
    active = jnp.where(me == 0, 0.0, 1.0).astype(jnp.float32)
    quarter = 3 * FR * ROWS // 4
    for k, part in enumerate((q0, q1, q2, q3)):
        at = lax.rem(lax.rem(me, 4) + 4 - k, 4)
        fringe[pl.ds(pl.multiple_of(at * quarter, ROWS), quarter), :] = part[...]
    row, lane = iotas()
    first_row, last_row = row == 0, row == ROWS - 1
    first_lane, last_lane = lane == 0, lane == NZ - 1

    for side in range(2):
        wait_all(planes[2 * side : 2 * side + 2])
        at = every8(side * (ROWS - 1))
        own, other = 2 * side, 2 * side + 1
        faces = 0.5 * (rims[own, 3] + rims[other, 3])
        for c in range(3):
            plane = out_ref[c, at, :] + faces * (rims[other, c] - rims[own, c])
            if c == 0:
                plane = plane - DRAG * disc_ref[side] * plane * jnp.abs(plane)
            out_ref[c, at, :] = plane
    start = start_ref[0]

    def blend(i, _):
        weight = profile_ref[i] * active
        for c in range(3):
            old = out_ref[c, tile(start + i), :]
            out_ref[c, tile(start + i), :] = old + weight * (fringe[tile(c * FR + i), :] - old)
        return 0

    lax.fori_loop(0, FR, blend, 0, unroll=8)
    for c in range(3):
        copies.append(pltpu.make_async_copy(out_ref.at[c], store.at[pl.ds(c * CELLS, CELLS)], sems.at[1 + c]))
        copies[-1].start()

    def source(x, carry):
        behind, now = carry
        ahead = out_ref[0, tile(lax.rem(x + 1, NX)), :]
        v = out_ref[1, tile(x), :]
        w = out_ref[2, tile(x), :]
        up = jnp.where(last_row, 0.0, pltpu.roll(v, ROWS - 1, 0))
        down = jnp.where(first_row, 0.0, pltpu.roll(v, 1, 0))
        div[tile(x), :] = 0.5 * ((ahead - behind) + (up - down) + centred_z(w, first_lane, last_lane))
        return now, ahead

    lax.fori_loop(0, NX, source, (out_ref[0, tile(NX - 1), :], out_ref[0, tile(0), :]), unroll=16)

    z_high, z_low = parts(table_ref[pl.ds(TAB_Z, NZ), :])
    for block in range(8):
        rows = pl.ds(block * NX, NX)
        modes[rows, :] = dot3(*parts(div[rows, :]), z_high, z_low)
    low = out_ref[1, every8(0), :]
    high = out_ref[1, every8(ROWS - 1), :]
    low_ref[...] = low
    high_ref[...] = high
    low = dot3(*parts(0.5 * low), z_high, z_low)
    high = dot3(*parts(-0.5 * high), z_high, z_low)
    x_high, x_low = parts(x_matrix(table_ref))
    for r in range(0, EXT, 2):
        pair = []
        for k in (r, r + 1):
            pair.append(low if k == 0 else high if k == EXT - 1 else modes[every8(k - 1), :])
        both = dot3(x_high, x_low, *parts(jnp.concatenate(pair, 1)))
        hat_ref[r] = both[:, :NZ]
        hat_ref[r + 1] = both[:, NZ:]
        for k in (r, r + 1):
            to = store.at[pl.ds(STORE_HAT + k * NX, NX)]
            copies.append(pltpu.make_async_copy(hat_ref.at[k], to, sems.at[4 + k]))
            copies[-1].start()

    origin = (row == 0) & (lane == 0)

    def sums(block, at):
        mu = table_ref[at, :]
        rows = [hat_ref[r, at, :] for r in range(EXT)]
        right = rows[0]
        for value in rows[1:]:
            right = mu * right + value
        left = rows[-1]
        for value in rows[-2::-1]:
            left = mu * left + value
        return right, left, rows

    def weigh(block, _):
        right, left, _ = sums(block, tile(block))
        pay_ref[block, 0] = right
        pay_ref[block, 1] = left
        return 0

    lax.fori_loop(1, NX // ROWS, weigh, 0, unroll=4)
    right, left, rows = sums(0, tile(0))
    moment0 = functools.reduce(jnp.add, rows)
    moment1 = functools.reduce(jnp.add, [float(r - 1) * rows[r] for r in range(EXT) if r != 1])
    pay_ref[0, 0] = jnp.where(origin, moment0, right)
    pay_ref[0, 1] = jnp.where(origin, moment1, left)
    wait_all(copies)


def far_kernel(pay_ref, step_ref, wrap_ref, out_ref):
    slab = lax.axis_index("slab")
    step = step_ref[tile(slab), :]
    wrap = wrap_ref[tile(slab), :]
    row, lane = iotas()
    origin = (row == 0) & (lane == 0) & (slab == 0)
    right = jnp.zeros((ROWS, NZ), jnp.float32)
    left = right
    total0 = right
    total1 = right
    ramp = right
    for s in range(SLABS):
        right = step * right + pay_ref[s, 0]
        left = step * left + pay_ref[SLABS - 1 - s, 1]
        total0 = total0 + pay_ref[s, 0]
        total1 = total1 + pay_ref[s, 1]
        ramp = ramp + float((SLABS - s) % SLABS) * pay_ref[s, 0]
    right = right * wrap
    left = left * wrap
    for s in range(SLABS):
        m0, m1 = pay_ref[s, 0], pay_ref[s, 1]
        if s:
            ramp = ramp + total0 - float(SLABS) * m0
        slope = 0.5 * (total0 - m0) - (ROWS / NY) * ramp + (1.0 / NY) * (total1 - m1)
        out_ref[s, 0] = jnp.where(origin, slope, right)
        right = step * right + m0
        t = SLABS - 1 - s
        curve = (-0.5 / NY) * (total0 - pay_ref[t, 0])
        out_ref[t, 1] = jnp.where(origin, curve, left)
        left = step * left + pay_ref[t, 1]


OUT_CHUNKS = 4


def green0(j):
    return 0.5 * j - j * j / (2.0 * NY)


def final_kernel(
    ret_ref, prev_ref, next_ref, store,
    out_hbm, press, field, rim, out_ref, field_ref, hat_ref, table_ref, sems, out_sems,
):
    hats = [(store.at[pl.ds(STORE_HAT + r * NX, NX)], hat_ref.at[r]) for r in range(EXT)]
    lines = (pl.ds(0, NX), pl.ds(NX, LATER - NX))
    later = [(store.at[pl.ds(STORE_LATER + s.start, s.size)], table_ref.at[s]) for s in lines]
    fields = [(store.at[pl.ds(c * CELLS, CELLS)], field_ref.at[c]) for c in range(3)]
    copies = start_all([later[0], *hats, later[1], *fields], sems)
    wait_all(copies[: 1 + EXT])
    row, lane = iotas()
    first_row, last_row = row == 0, row == ROWS - 1
    first_lane, last_lane = lane == 0, lane == NZ - 1
    origin = (row == 0) & (lane == 0)

    def solve(block, at):
        mu = table_ref[at, :]
        inv = 1.0 / jnp.where(mu == 0.0, 1.0, mu)
        scale = jnp.where(mu == 0.0, 0.0, -1.0 / ((1.0 + mu) * (1.0 - mu) * inv))
        rows = [hat_ref[r, at, :] for r in range(EXT)]
        below = [ret_ref[block, 0] * inv + rows[0]]
        for value in rows[1:]:
            below.append(mu * below[-1] + value)
        above = [ret_ref[block, 1] * inv]
        for value in rows[:0:-1]:
            above.append(mu * (above[-1] + value))
        above.reverse()
        return [scale * (a + b) for a, b in zip(below, above)], rows

    def line(block, _):
        at = tile(block)
        values, _ = solve(block, at)
        for r in range(EXT):
            press[r, at, :] = values[r]
        return 0

    lax.fori_loop(1, NX // ROWS, line, 0, unroll=4)
    at = pl.ds(0, ROWS)
    values, rows = solve(0, at)
    slope, curve = ret_ref[0, 0], ret_ref[0, 1]
    for r in range(EXT):
        y = float(r - 1)
        mean_line = slope * y + curve * (y * y)
        for k in range(EXT):
            if k != r:
                mean_line = mean_line + green0(float(abs(r - k))) * rows[k]
        press[r, at, :] = jnp.where(origin, mean_line, values[r])

    copies[1 + EXT].wait()
    x_high, x_low = parts(x_matrix(table_ref))
    z_high, z_low = parts(table_ref[pl.ds(TAB_Z, NZ), :])
    for r in range(0, EXT, 2):
        pair = jnp.concatenate([press[r], press[r + 1]], 1)
        both = dot3(x_high, x_low, *parts(pair))
        for k in (r, r + 1):
            plane = both[:, :NZ] if k == r else both[:, NZ:]
            plane = dot3(*parts(plane), z_high, z_low)
            if k == 0:
                rim[every8(0), :] = plane - 0.5 * prev_ref[...]
            elif k == EXT - 1:
                rim[every8(ROWS - 1), :] = plane + 0.5 * next_ref[...]
            else:
                field[every8(k - 1), :] = plane

    def project(x, carry):
        behind, now = carry
        ahead = field[tile(lax.rem(x + 1, NX)), :]
        edge = rim[tile(x), :]
        up = jnp.where(last_row, edge, pltpu.roll(now, ROWS - 1, 0))
        down = jnp.where(first_row, edge, pltpu.roll(now, 1, 0))
        grads = (ahead - behind, up - down, centred_z(now, first_lane, last_lane))
        for c in range(3):
            out_ref[c, tile(x), :] = field_ref[c, tile(x), :] - 0.5 * grads[c]
        return now, ahead

    carry = (field[tile(NX - 1), :], field[tile(0), :])
    wait_all(copies[2 + EXT :])
    copies = []
    part = CELLS // OUT_CHUNKS
    count = NX // OUT_CHUNKS
    for k in range(OUT_CHUNKS):
        carry = lax.fori_loop(k * count, (k + 1) * count, project, carry, unroll=16)
        rows = pl.ds(k * part, part)
        copies.append(pltpu.make_async_copy(out_ref.at[:, rows], out_hbm.at[:, rows], out_sems.at[k]))
        copies[-1].start()
    wait_all(copies)


def pick_kernel(which, count, *refs):
    *pieces, out_ref = refs[: count] + refs[-1:]
    me = lax.axis_index("sim")
    for k, piece in enumerate(pieces):

        @pl.when(which(me) == k)
        def _(piece=piece):
            out_ref[...] = piece[...]


def pick(name, which, pieces, *after):
    (out,) = call(
        functools.partial(pick_kernel, which, len(pieces)),
        [pieces[0].shape],
        name,
        in_specs=[VM] * len(pieces) + [HB] * len(after),
        nbytes=2**18,
    )(*pieces, *after)
    return out


def scatter_y(piece):
    came = [lax.ppermute(piece[k], "sim", [(0, k)]) for k in (1, 2, 3)]
    return pick("pick_y", lambda me: lax.rem(me, 4), [piece[0], *came])


def gather_y(mine):
    quarters = [mine]
    for k in (1, 2, 3):
        pairs = [(4 * z + i, 4 * z + (i + k) % 4) for z in range(2) for i in range(4)]
        quarters.append(lax.ppermute(mine, "sim", pairs))
    return quarters


def local(velocity, viscosity, turbines, fringe_start):
    vel = velocity.reshape(3, CELLS, NZ)
    visc = viscosity.reshape(CELLS, NZ)
    turb = turbines.reshape(CELLS, NZ)
    x_basis = x_table()[0]
    z_basis = z_table()
    mu, step, wrap = line_tables()
    table, later = (
        np.concatenate([mu, x[:, :NZ], x[:, NZ:], z]).astype(np.float32)
        for x, z in ((x_basis, z_basis.T), (x_basis.T, z_basis))
    )
    profile = (np.sin(math.pi * (np.arange(FR) + 0.5) / FR) ** 2).astype(np.float32)
    upward = [(i, (i + 1) % SLABS) for i in range(SLABS)]
    downward = [((i + 1) % SLABS, i) for i in range(SLABS)]

    f32 = jnp.float32
    quarter = (3 * FR * ROWS // 4, NZ)
    plane = (NX, NZ)
    *pieces, low, high = call(
        edges_kernel,
        [quarter] * 4 + [(4, NX, NZ)] * 2,
        "edges",
        room=60,
        in_specs=[SM, HB, HB],
        out_specs=[HB] * 6,
        scratch=[
            pltpu.VMEM((3, CELLS, NZ), f32),
            pltpu.VMEM((CELLS, NZ), f32),
            pltpu.VMEM((4, NX, NZ), f32),
            pltpu.VMEM((4, NX, NZ), f32),
            pltpu.SemaphoreType.DMA((2 * EDGE_CHUNKS,)),
            pltpu.SemaphoreType.DMA((2 * EDGE_CHUNKS,)),
            pltpu.SemaphoreType.DMA((6,)),
        ],
        nbytes=6 * 2**20,
    )(fringe_start, vel, visc)
    prev = lax.ppermute(high, "slab", upward)
    following = lax.ppermute(low, "slab", downward)

    mine = scatter_y(pieces)
    came = lax.ppermute(mine, "sim", [(i, i + 4) for i in range(4)])
    fields, discs = call(
        diffuse_kernel,
        [(3, CELLS, NZ), (2, NX, NZ)],
        "diffuse",
        room=DIFFUSE_ROOM,
        in_specs=[VM] * 3 + [HB],
        flops=2**26,
        nbytes=8 * 2**20,
    )(vel, visc, turb, mine)
    quarters = gather_y(pick("pick_z", lambda me: me // 4, [mine, came], discs))
    store, pay, v_low, v_high, _ = call(
        forward_kernel,
        [(STORE, NZ), (SLABS, 2, ROWS, NZ), plane, plane, (3, CELLS, NZ)],
        "forward",
        room=FORWARD_ROOM,
        in_specs=[SM] + [VM] * 2 + [HB] * 4 + [VM] * 4 + [SM] + [VM] * 2,
        out_specs=[HB, VM, VM, VM, VM],
        scratch=[
            pltpu.VMEM((4, 4, NX, NZ), f32),
            pltpu.VMEM((3 * FR * ROWS, NZ), f32),
            pltpu.VMEM((CELLS, NZ), f32),
            pltpu.VMEM((CELLS, NZ), f32),
            pltpu.VMEM((EXT, NX, NZ), f32),
            pltpu.SemaphoreType.DMA((4 + EXT,)),
            pltpu.SemaphoreType.DMA((4,)),
        ],
        flops=2**30,
        nbytes=10 * 2**20,
        input_output_aliases={1: 4},
    )(fringe_start, fields, discs, low, high, prev, following, *quarters, profile, table, later)
    v_prev = lax.ppermute(v_high, "slab", upward)
    v_next = lax.ppermute(v_low, "slab", downward)
    pay = lax.all_to_all(pay, "slab", split_axis=0, concat_axis=0, tiled=True)
    (ret,) = call(
        far_kernel,
        [(SLABS, 2, ROWS, NZ)],
        "far",
        in_specs=[VM] * 3,
        nbytes=2**19,
    )(pay, step, wrap)
    ret = lax.all_to_all(ret, "slab", split_axis=0, concat_axis=0, tiled=True)
    (out,) = call(
        final_kernel,
        [(3, CELLS, NZ)],
        "final",
        room=FORWARD_ROOM,
        in_specs=[VM, VM, VM, HB],
        out_specs=[HB],
        scratch=[
            pltpu.VMEM((EXT, NX, NZ), f32),
            pltpu.VMEM((CELLS, NZ), f32),
            pltpu.VMEM((CELLS, NZ), f32),
            pltpu.VMEM((3, CELLS, NZ), f32),
            pltpu.VMEM((3, CELLS, NZ), f32),
            pltpu.VMEM((EXT, NX, NZ), f32),
            pltpu.VMEM((LATER, NZ), f32),
            pltpu.SemaphoreType.DMA((5 + EXT,)),
            pltpu.SemaphoreType.DMA((OUT_CHUNKS,)),
        ],
        flops=2**30,
        nbytes=10 * 2**20,
    )(ret, v_prev, v_next, store)
    return out.reshape(velocity.shape)


def solution(mesh):
    return jax.shard_map(
        local,
        mesh=mesh,
        in_specs=(
            P("sim", None, None, "slab", None),
            P("sim", None, "slab", None),
            P("sim", None, "slab", None),
            P(),
        ),
        out_specs=P("sim", None, None, "slab", None),
        check_vma=False,
    )
```

```python
import functools
import math

import jax
import jax.numpy as jnp
import numpy as np
from jax import lax
from jax.experimental import pallas as pl
from jax.experimental.pallas import tpu as pltpu
from jax.sharding import PartitionSpec as P

FR = 32
NX = 256
NY = 256
NZ = 128
SLABS = 32
ROWS = 8
EXT = ROWS + 2
CELLS = NX * ROWS
DRAG = 0.5 * 0.75
MIB = 2**20
DIFFUSE_ROOM = 40
FORWARD_ROOM = 40


def x_table():
    half = NX // 2
    x = np.arange(NX)
    wave = np.concatenate([np.arange(half + 1), np.arange(1, half)])
    angle = 2.0 * math.pi / NX * ((wave[:, None] * x[None, :]) % NX)
    basis = np.where((np.arange(NX) <= half)[:, None], np.cos(angle), np.sin(angle))
    weight = np.where((wave == 0) | (wave == half), 1.0, 2.0) / NX
    return basis * np.sqrt(weight)[:, None], wave


def z_table():
    m = np.arange(NZ)
    angle = math.pi / (2.0 * NZ) * ((m[:, None] * (2 * m[None, :] + 1)) % (4 * NZ))
    weight = np.where(m == 0, 1.0, 2.0) / NZ
    return np.cos(angle) * np.sqrt(weight)[:, None]


def line_tables():
    wave = x_table()[1]
    minus_x = 4.0 * np.sin(math.pi * wave / NX) ** 2
    minus_z = 4.0 * np.sin(math.pi * np.arange(NZ) / (2.0 * NZ)) ** 2
    total = minus_x[:, None] + minus_z[None, :]
    theta = 2.0 * np.arcsinh(np.sqrt(total) / 2.0)
    zero = total == 0.0
    theta = np.where(zero, 1.0, theta)
    mu = np.exp(-theta)
    wrap = 1.0 / (-np.expm1(-NY * theta))
    tables = [mu, np.exp(-ROWS * theta), wrap]
    return [np.where(zero, 0.0, t).astype(np.float32) for t in tables]


def dot3(a_high, a_low, b_high, b_low):
    dot = functools.partial(jnp.dot, preferred_element_type=jnp.float32)
    return dot(a_high, b_high) + (dot(a_high, b_low) + dot(a_low, b_high))


def parts(value):
    high = value.astype(jnp.bfloat16)
    low = (value - high.astype(jnp.float32)).astype(jnp.bfloat16)
    return high, low


def call(body, outs, name, scratch=(), in_specs=None, out_specs=None, room=20, flops=0, nbytes=0, **kw):
    return pl.pallas_call(
        body,
        out_shape=[jax.ShapeDtypeStruct(s, jnp.float32) for s in outs],
        in_specs=in_specs,
        out_specs=out_specs or [VM] * len(outs),
        scratch_shapes=list(scratch),
        compiler_params=pltpu.CompilerParams(vmem_limit_bytes=room * MIB),
        cost_estimate=pl.CostEstimate(flops=flops, bytes_accessed=nbytes, transcendentals=0),
        name=name,
        **kw,
    )


VM = pl.BlockSpec(memory_space=pltpu.VMEM)
SM = pl.BlockSpec(memory_space=pltpu.SMEM)
HB = pl.BlockSpec(memory_space=pltpu.HBM)


def start_all(pairs, sems):
    copies = [pltpu.make_async_copy(a, b, sems.at[k]) for k, (a, b) in enumerate(pairs)]
    for copy in copies:
        copy.start()
    return copies


def wait_all(copies):
    for copy in copies:
        copy.wait()


def every8(first, count=NX):
    return pl.ds(first, count, stride=ROWS)


EDGE_CHUNKS = 4


def edges_kernel(
    start_ref, vel_in, visc_in, q0, q1, q2, q3, low_out, high_out,
    vel_ref, visc_ref, low_ref, high_ref, sems, out_sems, piece_sems,
):
    part = CELLS // EDGE_CHUNKS
    pairs = []
    for k in range(EDGE_CHUNKS):
        rows = pl.ds(k * part, part)
        pairs += [(vel_in.at[:, rows], vel_ref.at[:, rows]), (visc_in.at[rows], visc_ref.at[rows])]
    copies = start_all(pairs, sems)
    count = NX // EDGE_CHUNKS
    outs = []
    for k in range(EDGE_CHUNKS):
        wait_all(copies[2 * k : 2 * k + 2])
        planes = pl.ds(k * count, count)
        for row, out in ((0, low_ref), (ROWS - 1, high_ref)):
            for c in range(3):
                out[c, planes, :] = vel_ref[c, every8(k * part + row, count), :]
            out[3, planes, :] = visc_ref[every8(k * part + row, count), :]
        if k == EDGE_CHUNKS - 1:
            first = pl.multiple_of(start_ref[0] * ROWS, ROWS)
            rows = FR * ROWS
            quarter = 3 * rows // 4
            pairs = []
            for n, out in enumerate((q0, q1, q2, q3)):
                at = n * quarter
                while at < (n + 1) * quarter:
                    c, inner = divmod(at, rows)
                    size = min(rows - inner, (n + 1) * quarter - at)
                    from_rows, to_rows = pl.ds(first + inner, size), pl.ds(at - n * quarter, size)
                    pairs.append((vel_ref.at[c, from_rows], out.at[to_rows]))
                    at += size
            outs += start_all(pairs, piece_sems)
        for side, (plane, to) in enumerate(((low_ref, low_out), (high_ref, high_out))):
            outs.append(pltpu.make_async_copy(plane.at[:, planes], to.at[:, planes], out_sems.at[2 * k + side]))
            outs[-1].start()
    wait_all(outs)


def iotas():
    return (
        lax.broadcasted_iota(jnp.int32, (ROWS, NZ), 0),
        lax.broadcasted_iota(jnp.int32, (ROWS, NZ), 1),
    )


def tile(x):
    return pl.ds(pl.multiple_of(x * ROWS, ROWS), ROWS)


def diffuse_kernel(vel_ref, visc_ref, turb_ref, *refs):
    *_, out_ref, disc_ref = refs
    row, lane = iotas()
    last_row, last_lane = row == ROWS - 1, lane == NZ - 1
    inner = jnp.where((row == 0) | last_row, 0.0, DRAG).astype(jnp.float32)

    def fields_at(x):
        return [vel_ref[c, tile(x), :] for c in range(3)], visc_ref[tile(x), :]

    def step(x, carry):
        now, nu, back = carry
        ahead, nu_ahead = fields_at(lax.rem(x + 1, NX))
        half = 0.5 * nu
        sum_x = half + 0.5 * nu_ahead
        sum_y = jnp.where(last_row, 0.0, half + pltpu.roll(half, ROWS - 1, 0))
        sum_z = jnp.where(last_lane, 0.0, half + pltpu.roll(half, NZ - 1, 1))
        fluxes = []
        for c in range(3):
            u = now[c]
            flux_x = sum_x * (ahead[c] - u)
            flux_y = sum_y * (pltpu.roll(u, ROWS - 1, 0) - u)
            flux_z = sum_z * (pltpu.roll(u, NZ - 1, 1) - u)
            down_y, down_z = pltpu.roll(flux_y, 1, 0), pltpu.roll(flux_z, 1, 1)
            new = u + (flux_x - back[c]) + (flux_y - down_y) + (flux_z - down_z)
            if c == 0:
                disc = turb_ref[tile(x), :].astype(jnp.float32)
                new = new - inner * disc * new * jnp.abs(new)
            out_ref[c, tile(x), :] = new
            fluxes.append(flux_x)
        return ahead, nu_ahead, fluxes

    before, nu_before = fields_at(NX - 1)
    now, nu = fields_at(0)
    sum_x = 0.5 * nu_before + 0.5 * nu
    back = [sum_x * (now[c] - before[c]) for c in range(3)]
    lax.fori_loop(0, NX, step, (now, nu, back), unroll=16)
    for side, at in enumerate((0, ROWS - 1)):
        disc_ref[side] = turb_ref[every8(at), :].astype(jnp.float32)


def centred_z(value, first_lane, last_lane):
    up = jnp.where(last_lane, value, pltpu.roll(value, NZ - 1, 1))
    down = jnp.where(first_lane, value, pltpu.roll(value, 1, 1))
    return up - down


TAB_X = NX
TAB_Z = TAB_X + 2 * NX
LATER = TAB_Z + NZ
STORE_HAT = 3 * CELLS
STORE_LATER = STORE_HAT + EXT * NX
STORE = 40 * 2**11


def x_matrix(table_ref):
    return jnp.concatenate([table_ref[pl.ds(TAB_X, NX), :], table_ref[pl.ds(TAB_X + NX, NX), :]], 1)


def source_loop(read_x, v_ref, w_ref, out_ref, count, carry):
    row, lane = iotas()
    first_row, last_row = row == 0, row == ROWS - 1
    first_lane, last_lane = lane == 0, lane == NZ - 1

    def source(x, carry):
        behind, now = carry
        ahead = read_x(x)
        v, w = v_ref(x), w_ref(x)
        up = jnp.where(last_row, 0.0, pltpu.roll(v, ROWS - 1, 0))
        down = jnp.where(first_row, 0.0, pltpu.roll(v, 1, 0))
        out_ref[tile(x), :] = 0.5 * ((ahead - behind) + (up - down) + centred_z(w, first_lane, last_lane))
        return now, ahead

    lax.fori_loop(0, count, source, carry, unroll=16)


def forward_kernel(
    start_ref, field_ref, disc_ref, low_in, high_in, prev_in, next_in, after, profile_ref, table_ref, later_ref,
    store, hat_ref, low_ref, high_ref, out_ref, rims, div, modes, sems, rim_sems,
):
    del field_ref, after
    planes = start_all([(p, rims.at[k]) for k, p in enumerate((low_in, prev_in, high_in, next_in))], rim_sems)
    copies = start_all([(later_ref, store.at[pl.ds(STORE_LATER, LATER)])], sems)
    active = jnp.where(lax.axis_index("sim") == 0, 0.0, 1.0).astype(jnp.float32)

    for side in range(2):
        wait_all(planes[2 * side : 2 * side + 2])
        at = every8(side * (ROWS - 1))
        own, other = 2 * side, 2 * side + 1
        faces = 0.5 * (rims[own, 3] + rims[other, 3])
        for c in range(3):
            plane = out_ref[c, at, :] + faces * (rims[other, c] - rims[own, c])
            if c == 0:
                plane = plane - DRAG * disc_ref[side] * plane * jnp.abs(plane)
            out_ref[c, at, :] = plane
    start = start_ref[0]

    def blend(i, _):
        kept = 1.0 - profile_ref[i] * active
        for c in range(3):
            out_ref[c, tile(start + i), :] = kept * out_ref[c, tile(start + i), :]
        return 0

    lax.fori_loop(0, FR, blend, 0, unroll=8)
    for c in range(3):
        copies.append(pltpu.make_async_copy(out_ref.at[c], store.at[pl.ds(c * CELLS, CELLS)], sems.at[1 + c]))
        copies[-1].start()

    source_loop(
        lambda x: out_ref[0, tile(lax.rem(x + 1, NX)), :],
        lambda x: out_ref[1, tile(x), :],
        lambda x: out_ref[2, tile(x), :],
        div,
        NX,
        (out_ref[0, tile(NX - 1), :], out_ref[0, tile(0), :]),
    )
    z_high, z_low = parts(table_ref[pl.ds(TAB_Z, NZ), :])
    for block in range(8):
        rows = pl.ds(block * NX, NX)
        modes[rows, :] = dot3(*parts(div[rows, :]), z_high, z_low)
    low = out_ref[1, every8(0), :]
    high = out_ref[1, every8(ROWS - 1), :]
    low_ref[...] = low
    high_ref[...] = high
    low = dot3(*parts(0.5 * low), z_high, z_low)
    high = dot3(*parts(-0.5 * high), z_high, z_low)
    x_high, x_low = parts(x_matrix(table_ref))
    for r in range(0, EXT, 2):
        pair = []
        for k in (r, r + 1):
            pair.append(low if k == 0 else high if k == EXT - 1 else modes[every8(k - 1), :])
        both = dot3(x_high, x_low, *parts(jnp.concatenate(pair, 1)))
        hat_ref[r] = both[:, :NZ]
        hat_ref[r + 1] = both[:, NZ:]
    wait_all(copies)


WINDOW = 48
EDGE_WINDOW = FR + 8
TAB_WINDOW = NX + NZ
WINDOW_ROWS = NX + 2 * ROWS


def dot3_rows(a, b):
    dims = (((0,), (0,)), ((), ()))
    dot = functools.partial(lax.dot_general, dimension_numbers=dims, preferred_element_type=jnp.float32)
    (a_high, a_low), (b_high, b_low) = a, b
    return dot(a_high, b_high) + (dot(a_high, b_low) + dot(a_low, b_high))


def precursor_kernel(
    start_ref, q0, q1, q2, q3, profile_ref, hat_ref, low_ref, high_ref, table_ref, store_in,
    store, pay_ref, low_out, high_out, fringe, share, div, modes, rows_ref, edge, sums_ref, sems, row_sems,
):
    del store_in
    start = start_ref[0]
    me = lax.axis_index("sim")
    active = jnp.where(me == 0, 0.0, 1.0).astype(jnp.float32)
    length = FR * ROWS
    spans = [store.at[pl.ds(pl.multiple_of(c * CELLS + start * ROWS, ROWS), length)] for c in range(3)]
    loads = start_all([(span, rows_ref.at[c]) for c, span in enumerate(spans)], row_sems)
    quarter = 3 * length // 4
    for k, part in enumerate((q0, q1, q2, q3)):
        at = lax.rem(lax.rem(me, 4) + 4 - k, 4)
        fringe[pl.ds(pl.multiple_of(at * quarter, ROWS), quarter), :] = part[...]

    base = (start + 7) // 8 * 8 - 8
    offset = start - base
    share[...] = jnp.zeros_like(share)

    def weigh_rows(i, _):
        weight = profile_ref[i] * active
        for c in range(3):
            share[c, tile(i + offset + 1), :] = weight * fringe[tile(c * FR + i), :]
        return 0

    lax.fori_loop(0, FR, weigh_rows, 0, unroll=8)
    source_loop(
        lambda x: share[0, tile(x + 2), :],
        lambda x: share[1, tile(x + 1), :],
        lambda x: share[2, tile(x + 1), :],
        div,
        WINDOW,
        (share[0, tile(0), :], share[0, tile(1), :]),
    )
    z_high, z_low = parts(table_ref[pl.ds(NX, NZ), :])
    modes[...] = dot3(*parts(div[...]), z_high, z_low)
    ends = [share[1, every8(ROWS + y, WINDOW), :] for y in (0, ROWS - 1)]
    low = dot3(*parts(0.5 * ends[0]), z_high, z_low)
    high = dot3(*parts(-0.5 * ends[1]), z_high, z_low)
    at = pl.multiple_of(base + 8, ROWS)
    basis = parts(
        jnp.concatenate(
            [table_ref[pl.ds(TAB_WINDOW + half * WINDOW_ROWS + at, WINDOW), :] for half in range(2)], 1
        )
    )
    copies = []
    for r in range(0, EXT, 2):
        pair = []
        for k in (r, r + 1):
            pair.append(low if k == 0 else high if k == EXT - 1 else modes[every8(k - 1, WINDOW), :])
        both = dot3_rows(basis, parts(jnp.concatenate(pair, 1)))
        for k in (r, r + 1):
            sums_ref[k] = hat_ref[k] + (both[:, :NZ] if k == r else both[:, NZ:])
            to = store.at[pl.ds(STORE_HAT + k * NX, NX)]
            copies.append(pltpu.make_async_copy(sums_ref.at[k], to, sems.at[k]))
            copies[-1].start()

    wait_all(loads)

    def add_rows(i, _):
        for c in range(3):
            rows_ref[c, tile(i), :] = rows_ref[c, tile(i), :] + share[c, tile(i + offset + 1), :]
        return 0

    lax.fori_loop(0, FR, add_rows, 0, unroll=8)
    for c, span in enumerate(spans):
        copies.append(pltpu.make_async_copy(rows_ref.at[c], span, sems.at[EXT + c]))
        copies[-1].start()
    first = pl.multiple_of(start // 8 * 8, ROWS)
    for y, own, out in ((0, low_ref, low_out), (ROWS - 1, high_ref, high_out)):
        edge[pl.ds(0, NX), :] = own[...]
        to = pl.ds(first, EDGE_WINDOW)
        edge[to, :] = edge[to, :] + share[1, every8((first - base + 1) * ROWS + y, EDGE_WINDOW), :]
        out[...] = edge[pl.ds(0, NX), :]

    row, lane = iotas()
    origin = (row == 0) & (lane == 0)

    def sums(block, at):
        mu = table_ref[at, :]
        rows = [sums_ref[r, at, :] for r in range(EXT)]
        right = rows[0]
        for value in rows[1:]:
            right = mu * right + value
        left = rows[-1]
        for value in rows[-2::-1]:
            left = mu * left + value
        return right, left, rows

    def weigh(block, _):
        right, left, _ = sums(block, tile(block))
        pay_ref[block, 0] = right
        pay_ref[block, 1] = left
        return 0

    lax.fori_loop(1, NX // ROWS, weigh, 0, unroll=4)
    right, left, rows = sums(0, tile(0))
    moment0 = functools.reduce(jnp.add, rows)
    moment1 = functools.reduce(jnp.add, [float(r - 1) * rows[r] for r in range(EXT) if r != 1])
    pay_ref[0, 0] = jnp.where(origin, moment0, right)
    pay_ref[0, 1] = jnp.where(origin, moment1, left)
    wait_all(copies)


def far_kernel(pay_ref, step_ref, wrap_ref, out_ref):
    slab = lax.axis_index("slab")
    step = step_ref[tile(slab), :]
    wrap = wrap_ref[tile(slab), :]
    row, lane = iotas()
    origin = (row == 0) & (lane == 0) & (slab == 0)
    right = jnp.zeros((ROWS, NZ), jnp.float32)
    left = right
    total0 = right
    total1 = right
    ramp = right
    for s in range(SLABS):
        right = step * right + pay_ref[s, 0]
        left = step * left + pay_ref[SLABS - 1 - s, 1]
        total0 = total0 + pay_ref[s, 0]
        total1 = total1 + pay_ref[s, 1]
        ramp = ramp + float((SLABS - s) % SLABS) * pay_ref[s, 0]
    right = right * wrap
    left = left * wrap
    for s in range(SLABS):
        m0, m1 = pay_ref[s, 0], pay_ref[s, 1]
        if s:
            ramp = ramp + total0 - float(SLABS) * m0
        slope = 0.5 * (total0 - m0) - (ROWS / NY) * ramp + (1.0 / NY) * (total1 - m1)
        out_ref[s, 0] = jnp.where(origin, slope, right)
        right = step * right + m0
        t = SLABS - 1 - s
        curve = (-0.5 / NY) * (total0 - pay_ref[t, 0])
        out_ref[t, 1] = jnp.where(origin, curve, left)
        left = step * left + pay_ref[t, 1]


OUT_CHUNKS = 4


def green0(j):
    return 0.5 * j - j * j / (2.0 * NY)


def final_kernel(
    ret_ref, prev_ref, next_ref, store,
    out_hbm, press, field, rim, out_ref, field_ref, hat_ref, table_ref, sems, out_sems,
):
    hats = [(store.at[pl.ds(STORE_HAT + r * NX, NX)], hat_ref.at[r]) for r in range(EXT)]
    lines = (pl.ds(0, NX), pl.ds(NX, LATER - NX))
    later = [(store.at[pl.ds(STORE_LATER + s.start, s.size)], table_ref.at[s]) for s in lines]
    fields = [(store.at[pl.ds(c * CELLS, CELLS)], field_ref.at[c]) for c in range(3)]
    copies = start_all([later[0], *hats, later[1], *fields], sems)
    wait_all(copies[: 1 + EXT])
    row, lane = iotas()
    first_row, last_row = row == 0, row == ROWS - 1
    first_lane, last_lane = lane == 0, lane == NZ - 1
    origin = (row == 0) & (lane == 0)

    def solve(block, at):
        mu = table_ref[at, :]
        inv = 1.0 / jnp.where(mu == 0.0, 1.0, mu)
        scale = jnp.where(mu == 0.0, 0.0, -1.0 / ((1.0 + mu) * (1.0 - mu) * inv))
        rows = [hat_ref[r, at, :] for r in range(EXT)]
        below = [ret_ref[block, 0] * inv + rows[0]]
        for value in rows[1:]:
            below.append(mu * below[-1] + value)
        above = [ret_ref[block, 1] * inv]
        for value in rows[:0:-1]:
            above.append(mu * (above[-1] + value))
        above.reverse()
        return [scale * (a + b) for a, b in zip(below, above)], rows

    def line(block, _):
        at = tile(block)
        values, _ = solve(block, at)
        for r in range(EXT):
            press[r, at, :] = values[r]
        return 0

    lax.fori_loop(1, NX // ROWS, line, 0, unroll=4)
    at = pl.ds(0, ROWS)
    values, rows = solve(0, at)
    slope, curve = ret_ref[0, 0], ret_ref[0, 1]
    for r in range(EXT):
        y = float(r - 1)
        mean_line = slope * y + curve * (y * y)
        for k in range(EXT):
            if k != r:
                mean_line = mean_line + green0(float(abs(r - k))) * rows[k]
        press[r, at, :] = jnp.where(origin, mean_line, values[r])

    copies[1 + EXT].wait()
    x_high, x_low = parts(x_matrix(table_ref))
    z_high, z_low = parts(table_ref[pl.ds(TAB_Z, NZ), :])
    for r in range(0, EXT, 2):
        pair = jnp.concatenate([press[r], press[r + 1]], 1)
        both = dot3(x_high, x_low, *parts(pair))
        for k in (r, r + 1):
            plane = both[:, :NZ] if k == r else both[:, NZ:]
            plane = dot3(*parts(plane), z_high, z_low)
            if k == 0:
                rim[every8(0), :] = plane - 0.5 * prev_ref[...]
            elif k == EXT - 1:
                rim[every8(ROWS - 1), :] = plane + 0.5 * next_ref[...]
            else:
                field[every8(k - 1), :] = plane

    def project(x, carry):
        behind, now = carry
        ahead = field[tile(lax.rem(x + 1, NX)), :]
        edge = rim[tile(x), :]
        up = jnp.where(last_row, edge, pltpu.roll(now, ROWS - 1, 0))
        down = jnp.where(first_row, edge, pltpu.roll(now, 1, 0))
        grads = (ahead - behind, up - down, centred_z(now, first_lane, last_lane))
        for c in range(3):
            out_ref[c, tile(x), :] = field_ref[c, tile(x), :] - 0.5 * grads[c]
        return now, ahead

    carry = (field[tile(NX - 1), :], field[tile(0), :])
    wait_all(copies[2 + EXT :])
    copies = []
    part = CELLS // OUT_CHUNKS
    count = NX // OUT_CHUNKS
    for k in range(OUT_CHUNKS):
        carry = lax.fori_loop(k * count, (k + 1) * count, project, carry, unroll=16)
        rows = pl.ds(k * part, part)
        copies.append(pltpu.make_async_copy(out_ref.at[:, rows], out_hbm.at[:, rows], out_sems.at[k]))
        copies[-1].start()
    wait_all(copies)


def pick_kernel(which, count, *refs):
    *pieces, out_ref = refs[: count] + refs[-1:]
    me = lax.axis_index("sim")
    for k, piece in enumerate(pieces):

        @pl.when(which(me) == k)
        def _(piece=piece):
            out_ref[...] = piece[...]


def pick(name, which, pieces, *after):
    (out,) = call(
        functools.partial(pick_kernel, which, len(pieces)),
        [pieces[0].shape],
        name,
        in_specs=[VM] * len(pieces) + [HB] * len(after),
        nbytes=2**18,
    )(*pieces, *after)
    return out


def scatter_y(piece):
    came = [lax.ppermute(piece[k], "sim", [(0, k)]) for k in (1, 2, 3)]
    return pick("pick_y", lambda me: lax.rem(me, 4), [piece[0], *came])


def gather_y(mine):
    quarters = [mine]
    for k in (1, 2, 3):
        pairs = [(4 * z + i, 4 * z + (i + k) % 4) for z in range(2) for i in range(4)]
        quarters.append(lax.ppermute(mine, "sim", pairs))
    return quarters


def local(velocity, viscosity, turbines, fringe_start):
    vel = velocity.reshape(3, CELLS, NZ)
    visc = viscosity.reshape(CELLS, NZ)
    turb = turbines.reshape(CELLS, NZ)
    x_basis = x_table()[0]
    z_basis = z_table()
    mu, step, wrap = line_tables()
    table, later = (
        np.concatenate([mu, x[:, :NZ], x[:, NZ:], z]).astype(np.float32)
        for x, z in ((x_basis, z_basis.T), (x_basis.T, z_basis))
    )
    around = np.arange(-ROWS, NX + ROWS) % NX
    near = x_basis.T[around]
    near_table = np.concatenate([mu, z_basis.T, near[:, :NZ], near[:, NZ:]]).astype(np.float32)
    profile = (np.sin(math.pi * (np.arange(FR) + 0.5) / FR) ** 2).astype(np.float32)
    upward = [(i, (i + 1) % SLABS) for i in range(SLABS)]
    downward = [((i + 1) % SLABS, i) for i in range(SLABS)]

    f32 = jnp.float32
    quarter = (3 * FR * ROWS // 4, NZ)
    plane = (NX, NZ)
    *pieces, low, high = call(
        edges_kernel,
        [quarter] * 4 + [(4, NX, NZ)] * 2,
        "edges",
        room=60,
        in_specs=[SM, HB, HB],
        out_specs=[HB] * 6,
        scratch=[
            pltpu.VMEM((3, CELLS, NZ), f32),
            pltpu.VMEM((CELLS, NZ), f32),
            pltpu.VMEM((4, NX, NZ), f32),
            pltpu.VMEM((4, NX, NZ), f32),
            pltpu.SemaphoreType.DMA((2 * EDGE_CHUNKS,)),
            pltpu.SemaphoreType.DMA((2 * EDGE_CHUNKS,)),
            pltpu.SemaphoreType.DMA((6,)),
        ],
        nbytes=6 * 2**20,
    )(fringe_start, vel, visc)
    prev = lax.ppermute(high, "slab", upward)
    following = lax.ppermute(low, "slab", downward)

    mine = scatter_y(pieces)
    came = lax.ppermute(mine, "sim", [(i, i + 4) for i in range(4)])
    fields, discs = call(
        diffuse_kernel,
        [(3, CELLS, NZ), (2, NX, NZ)],
        "diffuse",
        room=DIFFUSE_ROOM,
        in_specs=[VM] * 3 + [HB],
        flops=2**26,
        nbytes=8 * 2**20,
    )(vel, visc, turb, mine)
    quarters = gather_y(pick("pick_z", lambda me: me // 4, [mine, came], discs))
    store, hat, v_low, v_high, _ = call(
        forward_kernel,
        [(STORE, NZ), (EXT, NX, NZ), plane, plane, (3, CELLS, NZ)],
        "forward",
        room=FORWARD_ROOM,
        in_specs=[SM] + [VM] * 2 + [HB] * 5 + [SM] + [VM] * 2,
        out_specs=[HB, VM, VM, VM, VM],
        scratch=[
            pltpu.VMEM((4, 4, NX, NZ), f32),
            pltpu.VMEM((CELLS, NZ), f32),
            pltpu.VMEM((CELLS, NZ), f32),
            pltpu.SemaphoreType.DMA((4,)),
            pltpu.SemaphoreType.DMA((4,)),
        ],
        flops=2**30,
        nbytes=10 * 2**20,
        input_output_aliases={1: 4},
    )(fringe_start, fields, discs, low, high, prev, following, quarters[0], profile, table, later)
    store, pay, v_low, v_high = call(
        precursor_kernel,
        [(STORE, NZ), (SLABS, 2, ROWS, NZ), plane, plane],
        "precursor",
        room=FORWARD_ROOM,
        in_specs=[SM] + [VM] * 4 + [SM] + [VM] * 4 + [HB],
        out_specs=[HB, VM, VM, VM],
        scratch=[
            pltpu.VMEM((3 * FR * ROWS, NZ), f32),
            pltpu.VMEM((3, (WINDOW + 2) * ROWS, NZ), f32),
            pltpu.VMEM((WINDOW * ROWS, NZ), f32),
            pltpu.VMEM((WINDOW * ROWS, NZ), f32),
            pltpu.VMEM((3, FR * ROWS, NZ), f32),
            pltpu.VMEM((NX + ROWS, NZ), f32),
            pltpu.VMEM((EXT, NX, NZ), f32),
            pltpu.SemaphoreType.DMA((EXT + 3,)),
            pltpu.SemaphoreType.DMA((3,)),
        ],
        flops=2**28,
        nbytes=3 * 2**20,
        input_output_aliases={10: 0},
    )(fringe_start, *quarters, profile, hat, v_low, v_high, near_table, store)
    v_prev = lax.ppermute(v_high, "slab", upward)
    v_next = lax.ppermute(v_low, "slab", downward)
    pay = lax.all_to_all(pay, "slab", split_axis=0, concat_axis=0, tiled=True)
    (ret,) = call(
        far_kernel,
        [(SLABS, 2, ROWS, NZ)],
        "far",
        in_specs=[VM] * 3,
        nbytes=2**19,
    )(pay, step, wrap)
    ret = lax.all_to_all(ret, "slab", split_axis=0, concat_axis=0, tiled=True)
    (out,) = call(
        final_kernel,
        [(3, CELLS, NZ)],
        "final",
        room=FORWARD_ROOM,
        in_specs=[VM, VM, VM, HB],
        out_specs=[HB],
        scratch=[
            pltpu.VMEM((EXT, NX, NZ), f32),
            pltpu.VMEM((CELLS, NZ), f32),
            pltpu.VMEM((CELLS, NZ), f32),
            pltpu.VMEM((3, CELLS, NZ), f32),
            pltpu.VMEM((3, CELLS, NZ), f32),
            pltpu.VMEM((EXT, NX, NZ), f32),
            pltpu.VMEM((LATER, NZ), f32),
            pltpu.SemaphoreType.DMA((5 + EXT,)),
            pltpu.SemaphoreType.DMA((OUT_CHUNKS,)),
        ],
        flops=2**30,
        nbytes=10 * 2**20,
    )(ret, v_prev, v_next, store)
    return out.reshape(velocity.shape)


def solution(mesh):
    return jax.shard_map(
        local,
        mesh=mesh,
        in_specs=(
            P("sim", None, None, "slab", None),
            P("sim", None, "slab", None),
            P("sim", None, "slab", None),
            P(),
        ),
        out_specs=P("sim", None, None, "slab", None),
        check_vma=False,
    )
```

```python
import functools
import math

import jax
import jax.numpy as jnp
import numpy as np
from jax import lax
from jax.experimental import pallas as pl
from jax.experimental.pallas import tpu as pltpu
from jax.sharding import PartitionSpec as P

FR = 32
NX = 256
NY = 256
NZ = 128
SLABS = 32
ROWS = 8
EXT = ROWS + 2
CELLS = NX * ROWS
DRAG = 0.5 * 0.75
MIB = 2**20
DIFFUSE_ROOM = 40
FORWARD_ROOM = 40


def x_table():
    half = NX // 2
    x = np.arange(NX)
    wave = np.concatenate([np.arange(half + 1), np.arange(1, half)])
    angle = 2.0 * math.pi / NX * ((wave[:, None] * x[None, :]) % NX)
    basis = np.where((np.arange(NX) <= half)[:, None], np.cos(angle), np.sin(angle))
    weight = np.where((wave == 0) | (wave == half), 1.0, 2.0) / NX
    return basis * np.sqrt(weight)[:, None], wave


def z_table():
    m = np.arange(NZ)
    angle = math.pi / (2.0 * NZ) * ((m[:, None] * (2 * m[None, :] + 1)) % (4 * NZ))
    weight = np.where(m == 0, 1.0, 2.0) / NZ
    return np.cos(angle) * np.sqrt(weight)[:, None]


def line_tables():
    wave = x_table()[1]
    minus_x = 4.0 * np.sin(math.pi * wave / NX) ** 2
    minus_z = 4.0 * np.sin(math.pi * np.arange(NZ) / (2.0 * NZ)) ** 2
    total = minus_x[:, None] + minus_z[None, :]
    theta = 2.0 * np.arcsinh(np.sqrt(total) / 2.0)
    zero = total == 0.0
    theta = np.where(zero, 1.0, theta)
    mu = np.exp(-theta)
    wrap = 1.0 / (-np.expm1(-NY * theta))
    tables = [mu, np.exp(-ROWS * theta), wrap]
    return [np.where(zero, 0.0, t).astype(np.float32) for t in tables]


def dot3(a_high, a_low, b_high, b_low):
    dot = functools.partial(jnp.dot, preferred_element_type=jnp.float32)
    return dot(a_high, b_high) + (dot(a_high, b_low) + dot(a_low, b_high))


def parts(value):
    high = value.astype(jnp.bfloat16)
    low = (value - high.astype(jnp.float32)).astype(jnp.bfloat16)
    return high, low


def twice(matrix):
    zero = jnp.zeros_like(matrix)
    return jnp.concatenate([jnp.concatenate([matrix, zero], 1), jnp.concatenate([zero, matrix], 1)], 0)


def halves(value):
    return value[:, :NZ], value[:, NZ:]


def call(body, outs, name, scratch=(), in_specs=None, out_specs=None, room=20, flops=0, nbytes=0, **kw):
    return pl.pallas_call(
        body,
        out_shape=[jax.ShapeDtypeStruct(s, jnp.float32) for s in outs],
        in_specs=in_specs,
        out_specs=out_specs or [VM] * len(outs),
        scratch_shapes=list(scratch),
        compiler_params=pltpu.CompilerParams(vmem_limit_bytes=room * MIB),
        cost_estimate=pl.CostEstimate(flops=flops, bytes_accessed=nbytes, transcendentals=0),
        name=name,
        **kw,
    )


VM = pl.BlockSpec(memory_space=pltpu.VMEM)
SM = pl.BlockSpec(memory_space=pltpu.SMEM)
HB = pl.BlockSpec(memory_space=pltpu.HBM)


def start_all(pairs, sems):
    copies = [pltpu.make_async_copy(a, b, sems.at[k]) for k, (a, b) in enumerate(pairs)]
    for copy in copies:
        copy.start()
    return copies


def wait_all(copies):
    for copy in copies:
        copy.wait()


def every8(first, count=NX):
    return pl.ds(first, count, stride=ROWS)


EDGE_CHUNKS = 4


def edges_kernel(
    start_ref, vel_in, visc_in, q0, q1, q2, q3, low_out, high_out,
    vel_ref, visc_ref, low_ref, high_ref, sems, out_sems, piece_sems,
):
    part = CELLS // EDGE_CHUNKS
    pairs = []
    for k in range(EDGE_CHUNKS):
        rows = pl.ds(k * part, part)
        pairs += [(vel_in.at[:, rows], vel_ref.at[:, rows]), (visc_in.at[rows], visc_ref.at[rows])]
    copies = start_all(pairs, sems)
    count = NX // EDGE_CHUNKS
    outs = []
    for k in range(EDGE_CHUNKS):
        wait_all(copies[2 * k : 2 * k + 2])
        planes = pl.ds(k * count, count)
        for row, out in ((0, low_ref), (ROWS - 1, high_ref)):
            for c in range(3):
                out[c, planes, :] = vel_ref[c, every8(k * part + row, count), :]
            out[3, planes, :] = visc_ref[every8(k * part + row, count), :]
        if k == EDGE_CHUNKS - 1:
            first = pl.multiple_of(start_ref[0] * ROWS, ROWS)
            rows = FR * ROWS
            quarter = 3 * rows // 4
            pairs = []
            for n, out in enumerate((q0, q1, q2, q3)):
                at = n * quarter
                while at < (n + 1) * quarter:
                    c, inner = divmod(at, rows)
                    size = min(rows - inner, (n + 1) * quarter - at)
                    from_rows, to_rows = pl.ds(first + inner, size), pl.ds(at - n * quarter, size)
                    pairs.append((vel_ref.at[c, from_rows], out.at[to_rows]))
                    at += size
            outs += start_all(pairs, piece_sems)
        for side, (plane, to) in enumerate(((low_ref, low_out), (high_ref, high_out))):
            outs.append(pltpu.make_async_copy(plane.at[:, planes], to.at[:, planes], out_sems.at[2 * k + side]))
            outs[-1].start()
    wait_all(outs)


def iotas():
    return (
        lax.broadcasted_iota(jnp.int32, (ROWS, NZ), 0),
        lax.broadcasted_iota(jnp.int32, (ROWS, NZ), 1),
    )


def tile(x):
    return pl.ds(pl.multiple_of(x * ROWS, ROWS), ROWS)


def diffuse_kernel(vel_ref, visc_ref, after, out_ref, done_ref):
    del after
    done_ref[...] = jnp.zeros_like(done_ref)
    row, lane = iotas()
    last_row, last_lane = row == ROWS - 1, lane == NZ - 1

    def fields_at(x):
        return [vel_ref[c, tile(x), :] for c in range(3)], visc_ref[tile(x), :]

    def step(x, carry):
        now, nu, back = carry
        ahead, nu_ahead = fields_at(lax.rem(x + 1, NX))
        half = 0.5 * nu
        sum_x = half + 0.5 * nu_ahead
        sum_y = jnp.where(last_row, 0.0, half + pltpu.roll(half, ROWS - 1, 0))
        sum_z = jnp.where(last_lane, 0.0, half + pltpu.roll(half, NZ - 1, 1))
        fluxes = []
        for c in range(3):
            u = now[c]
            flux_x = sum_x * (ahead[c] - u)
            flux_y = sum_y * (pltpu.roll(u, ROWS - 1, 0) - u)
            flux_z = sum_z * (pltpu.roll(u, NZ - 1, 1) - u)
            down_y, down_z = pltpu.roll(flux_y, 1, 0), pltpu.roll(flux_z, 1, 1)
            new = u + (flux_x - back[c]) + (flux_y - down_y) + (flux_z - down_z)
            out_ref[c, tile(x), :] = new
            fluxes.append(flux_x)
        return ahead, nu_ahead, fluxes

    before, nu_before = fields_at(NX - 1)
    now, nu = fields_at(0)
    sum_x = 0.5 * nu_before + 0.5 * nu
    back = [sum_x * (now[c] - before[c]) for c in range(3)]
    lax.fori_loop(0, NX, step, (now, nu, back), unroll=16)


def centred_z(value, first_lane, last_lane):
    up = jnp.where(last_lane, value, pltpu.roll(value, NZ - 1, 1))
    down = jnp.where(first_lane, value, pltpu.roll(value, 1, 1))
    return up - down


TAB_X = NX
TAB_Z = TAB_X + 2 * NX
LATER = TAB_Z + NZ
STORE_HAT = 3 * CELLS
STORE_LATER = STORE_HAT + EXT * NX
STORE = 40 * 2**11


def x_matrix(table_ref):
    return jnp.concatenate([table_ref[pl.ds(TAB_X, NX), :], table_ref[pl.ds(TAB_X + NX, NX), :]], 1)


def source_loop(read_x, v_ref, w_ref, out_ref, count, carry):
    row, lane = iotas()
    first_row, last_row = row == 0, row == ROWS - 1
    first_lane, last_lane = lane == 0, lane == NZ - 1

    def source(x, carry):
        behind, now = carry
        ahead = read_x(x)
        v, w = v_ref(x), w_ref(x)
        up = jnp.where(last_row, 0.0, pltpu.roll(v, ROWS - 1, 0))
        down = jnp.where(first_row, 0.0, pltpu.roll(v, 1, 0))
        out_ref[tile(x), :] = 0.5 * ((ahead - behind) + (up - down) + centred_z(w, first_lane, last_lane))
        return now, ahead

    lax.fori_loop(0, count, source, carry, unroll=16)


def forward_kernel(
    start_ref, field_ref, turb_ref, low_in, high_in, prev_in, next_in, after, profile_ref, table_ref, later_ref,
    store, hat_ref, low_ref, high_ref, out_ref, rims, div, modes, sems, rim_sems,
):
    del field_ref, after
    planes = start_all([(p, rims.at[k]) for k, p in enumerate((low_in, prev_in, high_in, next_in))], rim_sems)
    copies = start_all([(later_ref, store.at[pl.ds(STORE_LATER, LATER)])], sems)
    active = jnp.where(lax.axis_index("sim") == 0, 0.0, 1.0).astype(jnp.float32)

    for side in range(2):
        wait_all(planes[2 * side : 2 * side + 2])
        at = every8(side * (ROWS - 1))
        own, other = 2 * side, 2 * side + 1
        faces = 0.5 * (rims[own, 3] + rims[other, 3])
        for c in range(3):
            out_ref[c, at, :] = out_ref[c, at, :] + faces * (rims[other, c] - rims[own, c])
    start = start_ref[0]

    def drag(x, _):
        u = out_ref[0, tile(x), :]
        out_ref[0, tile(x), :] = u - DRAG * turb_ref[tile(x), :].astype(jnp.float32) * u * jnp.abs(u)
        return 0

    lax.fori_loop(0, NX, drag, 0, unroll=16)

    def blend(i, _):
        kept = 1.0 - profile_ref[i] * active
        for c in range(3):
            out_ref[c, tile(start + i), :] = kept * out_ref[c, tile(start + i), :]
        return 0

    lax.fori_loop(0, FR, blend, 0, unroll=8)
    for c in range(3):
        copies.append(pltpu.make_async_copy(out_ref.at[c], store.at[pl.ds(c * CELLS, CELLS)], sems.at[1 + c]))
        copies[-1].start()

    source_loop(
        lambda x: out_ref[0, tile(lax.rem(x + 1, NX)), :],
        lambda x: out_ref[1, tile(x), :],
        lambda x: out_ref[2, tile(x), :],
        div,
        NX,
        (out_ref[0, tile(NX - 1), :], out_ref[0, tile(0), :]),
    )
    z_high, z_low = parts(twice(table_ref[pl.ds(TAB_Z, NZ), :]))
    for block in range(0, ROWS, 2):
        first, second = pl.ds(block * NX, NX), pl.ds((block + 1) * NX, NX)
        pair = jnp.concatenate([div[first, :], div[second, :]], 1)
        modes[first, :], modes[second, :] = halves(dot3(*parts(pair), z_high, z_low))
    low = out_ref[1, every8(0), :]
    high = out_ref[1, every8(ROWS - 1), :]
    low_ref[...] = low
    high_ref[...] = high
    low, high = halves(dot3(*parts(jnp.concatenate([0.5 * low, -0.5 * high], 1)), z_high, z_low))
    x_high, x_low = parts(x_matrix(table_ref))
    for r in range(0, EXT, 2):
        pair = []
        for k in (r, r + 1):
            pair.append(low if k == 0 else high if k == EXT - 1 else modes[every8(k - 1), :])
        both = dot3(x_high, x_low, *parts(jnp.concatenate(pair, 1)))
        hat_ref[r] = both[:, :NZ]
        hat_ref[r + 1] = both[:, NZ:]
    wait_all(copies)


WINDOW = 48
EDGE_WINDOW = FR + 8
TAB_WINDOW = NX + NZ
WINDOW_ROWS = NX + 2 * ROWS


def dot3_rows(a, b):
    dims = (((0,), (0,)), ((), ()))
    dot = functools.partial(lax.dot_general, dimension_numbers=dims, preferred_element_type=jnp.float32)
    (a_high, a_low), (b_high, b_low) = a, b
    return dot(a_high, b_high) + (dot(a_high, b_low) + dot(a_low, b_high))


def precursor_kernel(
    start_ref, q0, q1, q2, q3, profile_ref, hat_ref, low_ref, high_ref, table_ref, store_in,
    store, pay_ref, low_out, high_out, fringe, share, div, modes, rows_ref, edge, sums_ref, sems, row_sems,
):
    del store_in
    start = start_ref[0]
    me = lax.axis_index("sim")
    active = jnp.where(me == 0, 0.0, 1.0).astype(jnp.float32)
    length = FR * ROWS
    spans = [store.at[pl.ds(pl.multiple_of(c * CELLS + start * ROWS, ROWS), length)] for c in range(3)]
    loads = start_all([(span, rows_ref.at[c]) for c, span in enumerate(spans)], row_sems)
    quarter = 3 * length // 4
    for k, part in enumerate((q0, q1, q2, q3)):
        at = lax.rem(lax.rem(me, 4) + 4 - k, 4)
        fringe[pl.ds(pl.multiple_of(at * quarter, ROWS), quarter), :] = part[...]

    base = (start + 7) // 8 * 8 - 8
    offset = start - base
    share[...] = jnp.zeros_like(share)

    def weigh_rows(i, _):
        weight = profile_ref[i] * active
        for c in range(3):
            share[c, tile(i + offset + 1), :] = weight * fringe[tile(c * FR + i), :]
        return 0

    lax.fori_loop(0, FR, weigh_rows, 0, unroll=8)
    source_loop(
        lambda x: share[0, tile(x + 2), :],
        lambda x: share[1, tile(x + 1), :],
        lambda x: share[2, tile(x + 1), :],
        div,
        WINDOW,
        (share[0, tile(0), :], share[0, tile(1), :]),
    )
    z_high, z_low = parts(twice(table_ref[pl.ds(NX, NZ), :]))
    half = WINDOW * ROWS // 2
    first, second = pl.ds(0, half), pl.ds(half, half)
    pair = jnp.concatenate([div[first, :], div[second, :]], 1)
    modes[first, :], modes[second, :] = halves(dot3(*parts(pair), z_high, z_low))
    ends = [share[1, every8(ROWS + y, WINDOW), :] for y in (0, ROWS - 1)]
    low, high = halves(dot3(*parts(jnp.concatenate([0.5 * ends[0], -0.5 * ends[1]], 1)), z_high, z_low))
    at = pl.multiple_of(base + 8, ROWS)
    basis = parts(
        jnp.concatenate(
            [table_ref[pl.ds(TAB_WINDOW + half * WINDOW_ROWS + at, WINDOW), :] for half in range(2)], 1
        )
    )
    copies = []
    for r in range(0, EXT, 2):
        pair = []
        for k in (r, r + 1):
            pair.append(low if k == 0 else high if k == EXT - 1 else modes[every8(k - 1, WINDOW), :])
        both = dot3_rows(basis, parts(jnp.concatenate(pair, 1)))
        for k in (r, r + 1):
            sums_ref[k] = hat_ref[k] + (both[:, :NZ] if k == r else both[:, NZ:])
            to = store.at[pl.ds(STORE_HAT + k * NX, NX)]
            copies.append(pltpu.make_async_copy(sums_ref.at[k], to, sems.at[k]))
            copies[-1].start()

    wait_all(loads)

    def add_rows(i, _):
        for c in range(3):
            rows_ref[c, tile(i), :] = rows_ref[c, tile(i), :] + share[c, tile(i + offset + 1), :]
        return 0

    lax.fori_loop(0, FR, add_rows, 0, unroll=8)
    for c, span in enumerate(spans):
        copies.append(pltpu.make_async_copy(rows_ref.at[c], span, sems.at[EXT + c]))
        copies[-1].start()
    first = pl.multiple_of(start // 8 * 8, ROWS)
    for y, own, out in ((0, low_ref, low_out), (ROWS - 1, high_ref, high_out)):
        edge[pl.ds(0, NX), :] = own[...]
        to = pl.ds(first, EDGE_WINDOW)
        edge[to, :] = edge[to, :] + share[1, every8((first - base + 1) * ROWS + y, EDGE_WINDOW), :]
        out[...] = edge[pl.ds(0, NX), :]

    row, lane = iotas()
    origin = (row == 0) & (lane == 0)

    def sums(block, at):
        mu = table_ref[at, :]
        rows = [sums_ref[r, at, :] for r in range(EXT)]
        right = rows[0]
        for value in rows[1:]:
            right = mu * right + value
        left = rows[-1]
        for value in rows[-2::-1]:
            left = mu * left + value
        return right, left, rows

    def weigh(block, _):
        right, left, _ = sums(block, tile(block))
        pay_ref[block, 0] = right
        pay_ref[block, 1] = left
        return 0

    lax.fori_loop(1, NX // ROWS, weigh, 0, unroll=4)
    right, left, rows = sums(0, tile(0))
    moment0 = functools.reduce(jnp.add, rows)
    moment1 = functools.reduce(jnp.add, [float(r - 1) * rows[r] for r in range(EXT) if r != 1])
    pay_ref[0, 0] = jnp.where(origin, moment0, right)
    pay_ref[0, 1] = jnp.where(origin, moment1, left)
    wait_all(copies)


def far_kernel(pay_ref, step_ref, wrap_ref, out_ref):
    slab = lax.axis_index("slab")
    step = step_ref[tile(slab), :]
    wrap = wrap_ref[tile(slab), :]
    row, lane = iotas()
    origin = (row == 0) & (lane == 0) & (slab == 0)
    right = jnp.zeros((ROWS, NZ), jnp.float32)
    left = right
    total0 = right
    total1 = right
    ramp = right
    for s in range(SLABS):
        right = step * right + pay_ref[s, 0]
        left = step * left + pay_ref[SLABS - 1 - s, 1]
        total0 = total0 + pay_ref[s, 0]
        total1 = total1 + pay_ref[s, 1]
        ramp = ramp + float((SLABS - s) % SLABS) * pay_ref[s, 0]
    right = right * wrap
    left = left * wrap
    for s in range(SLABS):
        m0, m1 = pay_ref[s, 0], pay_ref[s, 1]
        if s:
            ramp = ramp + total0 - float(SLABS) * m0
        slope = 0.5 * (total0 - m0) - (ROWS / NY) * ramp + (1.0 / NY) * (total1 - m1)
        out_ref[s, 0] = jnp.where(origin, slope, right)
        right = step * right + m0
        t = SLABS - 1 - s
        curve = (-0.5 / NY) * (total0 - pay_ref[t, 0])
        out_ref[t, 1] = jnp.where(origin, curve, left)
        left = step * left + pay_ref[t, 1]


OUT_CHUNKS = 8
HAT_CHUNKS = 4


def green0(j):
    return 0.5 * j - j * j / (2.0 * NY)


def final_kernel(
    ret_ref, prev_ref, next_ref, store,
    out_hbm, press, field, rim, out_ref, field_ref, hat_ref, table_ref, sems, out_sems,
):
    part = NX // HAT_CHUNKS
    hats = []
    for k in range(HAT_CHUNKS):
        hats += [(store.at[pl.ds(STORE_HAT + r * NX + k * part, part)], hat_ref.at[r, pl.ds(k * part, part)]) for r in range(EXT)]
    lines = (pl.ds(0, NX), pl.ds(NX, LATER - NX))
    later = [(store.at[pl.ds(STORE_LATER + s.start, s.size)], table_ref.at[s]) for s in lines]
    fields = [(store.at[pl.ds(c * CELLS, CELLS)], field_ref.at[c]) for c in range(3)]
    copies = start_all([later[0], *hats, later[1], *fields], sems)
    wait_all(copies[: 1 + EXT])
    copies = copies[1 + EXT :]
    row, lane = iotas()
    first_row, last_row = row == 0, row == ROWS - 1
    first_lane, last_lane = lane == 0, lane == NZ - 1
    origin = (row == 0) & (lane == 0)

    def solve(block, at):
        mu = table_ref[at, :]
        inv = 1.0 / jnp.where(mu == 0.0, 1.0, mu)
        scale = jnp.where(mu == 0.0, 0.0, -1.0 / ((1.0 + mu) * (1.0 - mu) * inv))
        rows = [hat_ref[r, at, :] for r in range(EXT)]
        below = [ret_ref[block, 0] * inv + rows[0]]
        for value in rows[1:]:
            below.append(mu * below[-1] + value)
        above = [ret_ref[block, 1] * inv]
        for value in rows[:0:-1]:
            above.append(mu * (above[-1] + value))
        above.reverse()
        return [scale * (a + b) for a, b in zip(below, above)], rows

    def line(block, _):
        at = tile(block)
        values, _ = solve(block, at)
        for r in range(EXT):
            press[r, at, :] = values[r]
        return 0

    count = part // ROWS
    for k in range(HAT_CHUNKS):
        if k:
            wait_all(copies[:EXT])
            copies = copies[EXT:]
        lax.fori_loop(k * count, (k + 1) * count, line, 0, unroll=4)
    at = pl.ds(0, ROWS)
    values, rows = solve(0, at)
    slope, curve = ret_ref[0, 0], ret_ref[0, 1]
    for r in range(EXT):
        y = float(r - 1)
        mean_line = slope * y + curve * (y * y)
        for k in range(EXT):
            if k != r:
                mean_line = mean_line + green0(float(abs(r - k))) * rows[k]
        press[r, at, :] = jnp.where(origin, mean_line, values[r])

    copies[0].wait()
    x_high, x_low = parts(x_matrix(table_ref))
    z_high, z_low = parts(twice(table_ref[pl.ds(TAB_Z, NZ), :]))
    for r in range(0, EXT, 2):
        pair = jnp.concatenate([press[r], press[r + 1]], 1)
        both = dot3(*parts(dot3(x_high, x_low, *parts(pair))), z_high, z_low)
        for k, plane in zip((r, r + 1), halves(both)):
            if k == 0:
                rim[every8(0), :] = plane - 0.5 * prev_ref[...]
            elif k == EXT - 1:
                rim[every8(ROWS - 1), :] = plane + 0.5 * next_ref[...]
            else:
                field[every8(k - 1), :] = plane

    def project(x, carry):
        behind, now = carry
        ahead = field[tile(lax.rem(x + 1, NX)), :]
        edge = rim[tile(x), :]
        up = jnp.where(last_row, edge, pltpu.roll(now, ROWS - 1, 0))
        down = jnp.where(first_row, edge, pltpu.roll(now, 1, 0))
        grads = (ahead - behind, up - down, centred_z(now, first_lane, last_lane))
        for c in range(3):
            out_ref[c, tile(x), :] = field_ref[c, tile(x), :] - 0.5 * grads[c]
        return now, ahead

    carry = (field[tile(NX - 1), :], field[tile(0), :])
    wait_all(copies[1:])
    copies = []
    part = CELLS // OUT_CHUNKS
    count = NX // OUT_CHUNKS
    for k in range(OUT_CHUNKS):
        carry = lax.fori_loop(k * count, (k + 1) * count, project, carry, unroll=16)
        rows = pl.ds(k * part, part)
        copies.append(pltpu.make_async_copy(out_ref.at[:, rows], out_hbm.at[:, rows], out_sems.at[k]))
        copies[-1].start()
    wait_all(copies)


def pick_kernel(which, count, *refs):
    *pieces, out_ref = refs[: count] + refs[-1:]
    me = lax.axis_index("sim")
    for k, piece in enumerate(pieces):

        @pl.when(which(me) == k)
        def _(piece=piece):
            out_ref[...] = piece[...]


def pick(name, which, pieces, *after):
    (out,) = call(
        functools.partial(pick_kernel, which, len(pieces)),
        [pieces[0].shape],
        name,
        in_specs=[VM] * len(pieces) + [HB] * len(after),
        nbytes=2**18,
    )(*pieces, *after)
    return out


def scatter_y(piece):
    came = [lax.ppermute(piece[k], "sim", [(0, k)]) for k in (1, 2, 3)]
    return pick("pick_y", lambda me: lax.rem(me, 4), [piece[0], *came])


def gather_y(mine):
    quarters = [mine]
    for k in (1, 2, 3):
        pairs = [(4 * z + i, 4 * z + (i + k) % 4) for z in range(2) for i in range(4)]
        quarters.append(lax.ppermute(mine, "sim", pairs))
    return quarters


def local(velocity, viscosity, turbines, fringe_start):
    vel = velocity.reshape(3, CELLS, NZ)
    visc = viscosity.reshape(CELLS, NZ)
    turb = turbines.reshape(CELLS, NZ)
    x_basis = x_table()[0]
    z_basis = z_table()
    mu, step, wrap = line_tables()
    table, later = (
        np.concatenate([mu, x[:, :NZ], x[:, NZ:], z]).astype(np.float32)
        for x, z in ((x_basis, z_basis.T), (x_basis.T, z_basis))
    )
    around = np.arange(-ROWS, NX + ROWS) % NX
    near = x_basis.T[around]
    near_table = np.concatenate([mu, z_basis.T, near[:, :NZ], near[:, NZ:]]).astype(np.float32)
    profile = (np.sin(math.pi * (np.arange(FR) + 0.5) / FR) ** 2).astype(np.float32)
    upward = [(i, (i + 1) % SLABS) for i in range(SLABS)]
    downward = [((i + 1) % SLABS, i) for i in range(SLABS)]

    f32 = jnp.float32
    quarter = (3 * FR * ROWS // 4, NZ)
    plane = (NX, NZ)
    *pieces, low, high = call(
        edges_kernel,
        [quarter] * 4 + [(4, NX, NZ)] * 2,
        "edges",
        room=60,
        in_specs=[SM, HB, HB],
        out_specs=[HB] * 6,
        scratch=[
            pltpu.VMEM((3, CELLS, NZ), f32),
            pltpu.VMEM((CELLS, NZ), f32),
            pltpu.VMEM((4, NX, NZ), f32),
            pltpu.VMEM((4, NX, NZ), f32),
            pltpu.SemaphoreType.DMA((2 * EDGE_CHUNKS,)),
            pltpu.SemaphoreType.DMA((2 * EDGE_CHUNKS,)),
            pltpu.SemaphoreType.DMA((6,)),
        ],
        nbytes=6 * 2**20,
    )(fringe_start, vel, visc)
    prev = lax.ppermute(high, "slab", upward)
    following = lax.ppermute(low, "slab", downward)

    mine = scatter_y(pieces)
    came = lax.ppermute(mine, "sim", [(i, i + 4) for i in range(4)])
    fields, done = call(
        diffuse_kernel,
        [(3, CELLS, NZ), (ROWS, NZ)],
        "diffuse",
        room=DIFFUSE_ROOM,
        in_specs=[VM] * 2 + [HB],
        flops=2**26,
        nbytes=8 * 2**20,
    )(vel, visc, mine)
    quarters = gather_y(pick("pick_z", lambda me: me // 4, [mine, came], done))
    store, hat, v_low, v_high, _ = call(
        forward_kernel,
        [(STORE, NZ), (EXT, NX, NZ), plane, plane, (3, CELLS, NZ)],
        "forward",
        room=FORWARD_ROOM,
        in_specs=[SM] + [VM] * 2 + [HB] * 5 + [SM] + [VM] * 2,
        out_specs=[HB, VM, VM, VM, VM],
        scratch=[
            pltpu.VMEM((4, 4, NX, NZ), f32),
            pltpu.VMEM((CELLS, NZ), f32),
            pltpu.VMEM((CELLS, NZ), f32),
            pltpu.SemaphoreType.DMA((4,)),
            pltpu.SemaphoreType.DMA((4,)),
        ],
        flops=2**30,
        nbytes=10 * 2**20,
        input_output_aliases={1: 4},
    )(fringe_start, fields, turb, low, high, prev, following, quarters[0], profile, table, later)
    store, pay, v_low, v_high = call(
        precursor_kernel,
        [(STORE, NZ), (SLABS, 2, ROWS, NZ), plane, plane],
        "precursor",
        room=FORWARD_ROOM,
        in_specs=[SM] + [VM] * 4 + [SM] + [VM] * 4 + [HB],
        out_specs=[HB, VM, VM, VM],
        scratch=[
            pltpu.VMEM((3 * FR * ROWS, NZ), f32),
            pltpu.VMEM((3, (WINDOW + 2) * ROWS, NZ), f32),
            pltpu.VMEM((WINDOW * ROWS, NZ), f32),
            pltpu.VMEM((WINDOW * ROWS, NZ), f32),
            pltpu.VMEM((3, FR * ROWS, NZ), f32),
            pltpu.VMEM((NX + ROWS, NZ), f32),
            pltpu.VMEM((EXT, NX, NZ), f32),
            pltpu.SemaphoreType.DMA((EXT + 3,)),
            pltpu.SemaphoreType.DMA((3,)),
        ],
        flops=2**28,
        nbytes=3 * 2**20,
        input_output_aliases={10: 0},
    )(fringe_start, *quarters, profile, hat, v_low, v_high, near_table, store)
    v_prev = lax.ppermute(v_high, "slab", upward)
    v_next = lax.ppermute(v_low, "slab", downward)
    pay = lax.all_to_all(pay, "slab", split_axis=0, concat_axis=0, tiled=True)
    (ret,) = call(
        far_kernel,
        [(SLABS, 2, ROWS, NZ)],
        "far",
        in_specs=[VM] * 3,
        nbytes=2**19,
    )(pay, step, wrap)
    ret = lax.all_to_all(ret, "slab", split_axis=0, concat_axis=0, tiled=True)
    (out,) = call(
        final_kernel,
        [(3, CELLS, NZ)],
        "final",
        room=FORWARD_ROOM,
        in_specs=[VM, VM, VM, HB],
        out_specs=[HB],
        scratch=[
            pltpu.VMEM((EXT, NX, NZ), f32),
            pltpu.VMEM((CELLS, NZ), f32),
            pltpu.VMEM((CELLS, NZ), f32),
            pltpu.VMEM((3, CELLS, NZ), f32),
            pltpu.VMEM((3, CELLS, NZ), f32),
            pltpu.VMEM((EXT, NX, NZ), f32),
            pltpu.VMEM((LATER, NZ), f32),
            pltpu.SemaphoreType.DMA((5 + HAT_CHUNKS * EXT,)),
            pltpu.SemaphoreType.DMA((OUT_CHUNKS,)),
        ],
        flops=2**30,
        nbytes=10 * 2**20,
    )(ret, v_prev, v_next, store)
    return out.reshape(velocity.shape)


def solution(mesh):
    return jax.shard_map(
        local,
        mesh=mesh,
        in_specs=(
            P("sim", None, None, "slab", None),
            P("sim", None, "slab", None),
            P("sim", None, "slab", None),
            P(),
        ),
        out_specs=P("sim", None, None, "slab", None),
        check_vma=False,
    )
```

```python
import functools
import math

import jax
import jax.numpy as jnp
import numpy as np
from jax import lax
from jax.experimental import pallas as pl
from jax.experimental.pallas import tpu as pltpu
from jax.sharding import PartitionSpec as P

FR = 32
NX = 256
NY = 256
NZ = 128
SLABS = 32
ROWS = 8
EXT = ROWS + 2
CELLS = NX * ROWS
DRAG = 0.5 * 0.75
MIB = 2**20
DIFFUSE_ROOM = 40
FORWARD_ROOM = 40


def x_table():
    half = NX // 2
    x = np.arange(NX)
    wave = np.concatenate([np.arange(half + 1), np.arange(1, half)])
    angle = 2.0 * math.pi / NX * ((wave[:, None] * x[None, :]) % NX)
    basis = np.where((np.arange(NX) <= half)[:, None], np.cos(angle), np.sin(angle))
    weight = np.where((wave == 0) | (wave == half), 1.0, 2.0) / NX
    return basis * np.sqrt(weight)[:, None], wave


def z_table():
    m = np.arange(NZ)
    angle = math.pi / (2.0 * NZ) * ((m[:, None] * (2 * m[None, :] + 1)) % (4 * NZ))
    weight = np.where(m == 0, 1.0, 2.0) / NZ
    return np.cos(angle) * np.sqrt(weight)[:, None]


def line_tables():
    wave = x_table()[1]
    minus_x = 4.0 * np.sin(math.pi * wave / NX) ** 2
    minus_z = 4.0 * np.sin(math.pi * np.arange(NZ) / (2.0 * NZ)) ** 2
    total = minus_x[:, None] + minus_z[None, :]
    theta = 2.0 * np.arcsinh(np.sqrt(total) / 2.0)
    zero = total == 0.0
    theta = np.where(zero, 1.0, theta)
    mu = np.exp(-theta)
    wrap = 1.0 / (-np.expm1(-NY * theta))
    tables = [mu, np.exp(-ROWS * theta), wrap]
    return [np.where(zero, 0.0, t).astype(np.float32) for t in tables]


def dot3(a_high, a_low, b_high, b_low):
    dot = functools.partial(jnp.dot, preferred_element_type=jnp.float32)
    return dot(a_high, b_high) + (dot(a_high, b_low) + dot(a_low, b_high))


def parts(value):
    high = value.astype(jnp.bfloat16)
    low = (value - high.astype(jnp.float32)).astype(jnp.bfloat16)
    return high, low


def twice(matrix):
    zero = jnp.zeros_like(matrix)
    return jnp.concatenate([jnp.concatenate([matrix, zero], 1), jnp.concatenate([zero, matrix], 1)], 0)


def halves(value):
    return value[:, :NZ], value[:, NZ:]


def call(body, outs, name, scratch=(), in_specs=None, out_specs=None, room=20, flops=0, nbytes=0, **kw):
    return pl.pallas_call(
        body,
        out_shape=[jax.ShapeDtypeStruct(s, jnp.float32) for s in outs],
        in_specs=in_specs,
        out_specs=out_specs or [VM] * len(outs),
        scratch_shapes=list(scratch),
        compiler_params=pltpu.CompilerParams(vmem_limit_bytes=room * MIB),
        cost_estimate=pl.CostEstimate(flops=flops, bytes_accessed=nbytes, transcendentals=0),
        name=name,
        **kw,
    )


VM = pl.BlockSpec(memory_space=pltpu.VMEM)
SM = pl.BlockSpec(memory_space=pltpu.SMEM)
HB = pl.BlockSpec(memory_space=pltpu.HBM)


def start_all(pairs, sems):
    copies = [pltpu.make_async_copy(a, b, sems.at[k]) for k, (a, b) in enumerate(pairs)]
    for copy in copies:
        copy.start()
    return copies


def wait_all(copies):
    for copy in copies:
        copy.wait()


def every8(first, count=NX):
    return pl.ds(first, count, stride=ROWS)


EDGE_CHUNKS = 4


def edges_kernel(
    start_ref, vel_in, visc_in, q0, q1, q2, q3, low_out, high_out,
    vel_ref, visc_ref, low_ref, high_ref, sems, out_sems, piece_sems,
):
    part = CELLS // EDGE_CHUNKS
    pairs = []
    for k in range(EDGE_CHUNKS):
        rows = pl.ds(k * part, part)
        pairs += [(vel_in.at[:, rows], vel_ref.at[:, rows]), (visc_in.at[rows], visc_ref.at[rows])]
    copies = start_all(pairs, sems)
    count = NX // EDGE_CHUNKS
    outs = []
    for k in range(EDGE_CHUNKS):
        wait_all(copies[2 * k : 2 * k + 2])
        planes = pl.ds(k * count, count)
        for row, out in ((0, low_ref), (ROWS - 1, high_ref)):
            for c in range(3):
                out[c, planes, :] = vel_ref[c, every8(k * part + row, count), :]
            out[3, planes, :] = visc_ref[every8(k * part + row, count), :]
        if k == EDGE_CHUNKS - 1:
            first = pl.multiple_of(start_ref[0] * ROWS, ROWS)
            rows = FR * ROWS
            quarter = 3 * rows // 4
            pairs = []
            for n, out in enumerate((q0, q1, q2, q3)):
                at = n * quarter
                while at < (n + 1) * quarter:
                    c, inner = divmod(at, rows)
                    size = min(rows - inner, (n + 1) * quarter - at)
                    from_rows, to_rows = pl.ds(first + inner, size), pl.ds(at - n * quarter, size)
                    pairs.append((vel_ref.at[c, from_rows], out.at[to_rows]))
                    at += size
            outs += start_all(pairs, piece_sems)
        for side, (plane, to) in enumerate(((low_ref, low_out), (high_ref, high_out))):
            outs.append(pltpu.make_async_copy(plane.at[:, planes], to.at[:, planes], out_sems.at[2 * k + side]))
            outs[-1].start()
    wait_all(outs)


def iotas():
    return (
        lax.broadcasted_iota(jnp.int32, (ROWS, NZ), 0),
        lax.broadcasted_iota(jnp.int32, (ROWS, NZ), 1),
    )


def tile(x):
    return pl.ds(pl.multiple_of(x * ROWS, ROWS), ROWS)


def diffuse_kernel(vel_ref, visc_ref, after, out_ref, done_ref):
    del after
    done_ref[...] = jnp.zeros_like(done_ref)
    row, lane = iotas()
    last_row, last_lane = row == ROWS - 1, lane == NZ - 1

    def fields_at(x):
        return [vel_ref[c, tile(x), :] for c in range(3)], visc_ref[tile(x), :]

    def step(x, carry):
        now, nu, back = carry
        ahead, nu_ahead = fields_at(lax.rem(x + 1, NX))
        half = 0.5 * nu
        sum_x = half + 0.5 * nu_ahead
        sum_y = jnp.where(last_row, 0.0, half + pltpu.roll(half, ROWS - 1, 0))
        sum_z = jnp.where(last_lane, 0.0, half + pltpu.roll(half, NZ - 1, 1))
        fluxes = []
        for c in range(3):
            u = now[c]
            flux_x = sum_x * (ahead[c] - u)
            flux_y = sum_y * (pltpu.roll(u, ROWS - 1, 0) - u)
            flux_z = sum_z * (pltpu.roll(u, NZ - 1, 1) - u)
            down_y, down_z = pltpu.roll(flux_y, 1, 0), pltpu.roll(flux_z, 1, 1)
            new = u + (flux_x - back[c]) + (flux_y - down_y) + (flux_z - down_z)
            out_ref[c, tile(x), :] = new
            fluxes.append(flux_x)
        return ahead, nu_ahead, fluxes

    before, nu_before = fields_at(NX - 1)
    now, nu = fields_at(0)
    sum_x = 0.5 * nu_before + 0.5 * nu
    back = [sum_x * (now[c] - before[c]) for c in range(3)]
    lax.fori_loop(0, NX, step, (now, nu, back), unroll=16)


def centred_z(value, first_lane, last_lane):
    up = jnp.where(last_lane, value, pltpu.roll(value, NZ - 1, 1))
    down = jnp.where(first_lane, value, pltpu.roll(value, 1, 1))
    return up - down


TAB_X = NX
TAB_Z = TAB_X + 2 * NX
LATER = TAB_Z + NZ
STORE_HAT = 3 * CELLS
STORE_LATER = STORE_HAT + EXT * NX
STORE = 40 * 2**11


def x_matrix(table_ref):
    return jnp.concatenate([table_ref[pl.ds(TAB_X, NX), :], table_ref[pl.ds(TAB_X + NX, NX), :]], 1)


def source_loop(read_x, v_ref, w_ref, out_ref, count, carry):
    row, lane = iotas()
    first_row, last_row = row == 0, row == ROWS - 1
    first_lane, last_lane = lane == 0, lane == NZ - 1

    def source(x, carry):
        behind, now = carry
        ahead = read_x(x)
        v, w = v_ref(x), w_ref(x)
        up = jnp.where(last_row, 0.0, pltpu.roll(v, ROWS - 1, 0))
        down = jnp.where(first_row, 0.0, pltpu.roll(v, 1, 0))
        out_ref[tile(x), :] = 0.5 * ((ahead - behind) + (up - down) + centred_z(w, first_lane, last_lane))
        return now, ahead

    lax.fori_loop(0, count, source, carry, unroll=16)


def forward_kernel(
    start_ref, field_ref, turb_ref, low_in, high_in, prev_in, next_in, after, profile_ref, table_ref, later_ref,
    store, hat_ref, low_ref, high_ref, out_ref, rims, div, modes, sems, rim_sems,
):
    del field_ref, after
    planes = start_all([(p, rims.at[k]) for k, p in enumerate((low_in, prev_in, high_in, next_in))], rim_sems)
    copies = start_all([(later_ref, store.at[pl.ds(STORE_LATER, LATER)])], sems)
    active = jnp.where(lax.axis_index("sim") == 0, 0.0, 1.0).astype(jnp.float32)

    for side in range(2):
        wait_all(planes[2 * side : 2 * side + 2])
        at = every8(side * (ROWS - 1))
        own, other = 2 * side, 2 * side + 1
        faces = 0.5 * (rims[own, 3] + rims[other, 3])
        for c in range(3):
            out_ref[c, at, :] = out_ref[c, at, :] + faces * (rims[other, c] - rims[own, c])
    start = start_ref[0]

    def drag(x, _):
        u = out_ref[0, tile(x), :]
        out_ref[0, tile(x), :] = u - DRAG * turb_ref[tile(x), :].astype(jnp.float32) * u * jnp.abs(u)
        return 0

    lax.fori_loop(0, NX, drag, 0, unroll=32)

    def blend(i, _):
        kept = 1.0 - profile_ref[i] * active
        for c in range(3):
            out_ref[c, tile(start + i), :] = kept * out_ref[c, tile(start + i), :]
        return 0

    lax.fori_loop(0, FR, blend, 0, unroll=16)
    for c in range(3):
        copies.append(pltpu.make_async_copy(out_ref.at[c], store.at[pl.ds(c * CELLS, CELLS)], sems.at[1 + c]))
        copies[-1].start()

    source_loop(
        lambda x: out_ref[0, tile(lax.rem(x + 1, NX)), :],
        lambda x: out_ref[1, tile(x), :],
        lambda x: out_ref[2, tile(x), :],
        div,
        NX,
        (out_ref[0, tile(NX - 1), :], out_ref[0, tile(0), :]),
    )
    z_high, z_low = parts(twice(table_ref[pl.ds(TAB_Z, NZ), :]))
    for block in range(0, ROWS, 2):
        first, second = pl.ds(block * NX, NX), pl.ds((block + 1) * NX, NX)
        pair = jnp.concatenate([div[first, :], div[second, :]], 1)
        modes[first, :], modes[second, :] = halves(dot3(*parts(pair), z_high, z_low))
    low = out_ref[1, every8(0), :]
    high = out_ref[1, every8(ROWS - 1), :]
    low_ref[...] = low
    high_ref[...] = high
    low, high = halves(dot3(*parts(jnp.concatenate([0.5 * low, -0.5 * high], 1)), z_high, z_low))
    x_high, x_low = parts(x_matrix(table_ref))
    for r in range(0, EXT, 2):
        pair = []
        for k in (r, r + 1):
            pair.append(low if k == 0 else high if k == EXT - 1 else modes[every8(k - 1), :])
        both = dot3(x_high, x_low, *parts(jnp.concatenate(pair, 1)))
        hat_ref[r] = both[:, :NZ]
        hat_ref[r + 1] = both[:, NZ:]
    wait_all(copies)


WINDOW = 48
EDGE_WINDOW = FR + 8
TAB_WINDOW = NX + NZ
WINDOW_ROWS = NX + 2 * ROWS


def dot3_rows(a, b):
    dims = (((0,), (0,)), ((), ()))
    dot = functools.partial(lax.dot_general, dimension_numbers=dims, preferred_element_type=jnp.float32)
    (a_high, a_low), (b_high, b_low) = a, b
    return dot(a_high, b_high) + (dot(a_high, b_low) + dot(a_low, b_high))


def precursor_kernel(
    start_ref, q0, q1, q2, q3, profile_ref, hat_ref, low_ref, high_ref, table_ref, store_in,
    store, pay_ref, low_out, high_out, fringe, share, div, modes, rows_ref, edge, sums_ref, sems, row_sems,
):
    del store_in
    start = start_ref[0]
    me = lax.axis_index("sim")
    active = jnp.where(me == 0, 0.0, 1.0).astype(jnp.float32)
    length = FR * ROWS
    spans = [store.at[pl.ds(pl.multiple_of(c * CELLS + start * ROWS, ROWS), length)] for c in range(3)]
    loads = start_all([(span, rows_ref.at[c]) for c, span in enumerate(spans)], row_sems)
    quarter = 3 * length // 4
    for k, part in enumerate((q0, q1, q2, q3)):
        at = lax.rem(lax.rem(me, 4) + 4 - k, 4)
        fringe[pl.ds(pl.multiple_of(at * quarter, ROWS), quarter), :] = part[...]

    base = (start + 7) // 8 * 8 - 8
    offset = start - base
    share[...] = jnp.zeros_like(share)

    def weigh_rows(i, _):
        weight = profile_ref[i] * active
        for c in range(3):
            share[c, tile(i + offset + 1), :] = weight * fringe[tile(c * FR + i), :]
        return 0

    lax.fori_loop(0, FR, weigh_rows, 0, unroll=8)
    source_loop(
        lambda x: share[0, tile(x + 2), :],
        lambda x: share[1, tile(x + 1), :],
        lambda x: share[2, tile(x + 1), :],
        div,
        WINDOW,
        (share[0, tile(0), :], share[0, tile(1), :]),
    )
    z_high, z_low = parts(twice(table_ref[pl.ds(NX, NZ), :]))
    half = WINDOW * ROWS // 2
    first, second = pl.ds(0, half), pl.ds(half, half)
    pair = jnp.concatenate([div[first, :], div[second, :]], 1)
    modes[first, :], modes[second, :] = halves(dot3(*parts(pair), z_high, z_low))
    ends = [share[1, every8(ROWS + y, WINDOW), :] for y in (0, ROWS - 1)]
    low, high = halves(dot3(*parts(jnp.concatenate([0.5 * ends[0], -0.5 * ends[1]], 1)), z_high, z_low))
    at = pl.multiple_of(base + 8, ROWS)
    basis = parts(
        jnp.concatenate(
            [table_ref[pl.ds(TAB_WINDOW + half * WINDOW_ROWS + at, WINDOW), :] for half in range(2)], 1
        )
    )
    copies = []
    for r in range(0, EXT, 2):
        pair = []
        for k in (r, r + 1):
            pair.append(low if k == 0 else high if k == EXT - 1 else modes[every8(k - 1, WINDOW), :])
        both = dot3_rows(basis, parts(jnp.concatenate(pair, 1)))
        for k in (r, r + 1):
            sums_ref[k] = hat_ref[k] + (both[:, :NZ] if k == r else both[:, NZ:])
            to = store.at[pl.ds(STORE_HAT + k * NX, NX)]
            copies.append(pltpu.make_async_copy(sums_ref.at[k], to, sems.at[k]))
            copies[-1].start()

    wait_all(loads)

    def add_rows(i, _):
        for c in range(3):
            rows_ref[c, tile(i), :] = rows_ref[c, tile(i), :] + share[c, tile(i + offset + 1), :]
        return 0

    lax.fori_loop(0, FR, add_rows, 0, unroll=8)
    for c, span in enumerate(spans):
        copies.append(pltpu.make_async_copy(rows_ref.at[c], span, sems.at[EXT + c]))
        copies[-1].start()
    first = pl.multiple_of(start // 8 * 8, ROWS)
    for y, own, out in ((0, low_ref, low_out), (ROWS - 1, high_ref, high_out)):
        edge[pl.ds(0, NX), :] = own[...]
        to = pl.ds(first, EDGE_WINDOW)
        edge[to, :] = edge[to, :] + share[1, every8((first - base + 1) * ROWS + y, EDGE_WINDOW), :]
        out[...] = edge[pl.ds(0, NX), :]

    row, lane = iotas()
    origin = (row == 0) & (lane == 0)

    def sums(block, at):
        mu = table_ref[at, :]
        rows = [sums_ref[r, at, :] for r in range(EXT)]
        right = rows[0]
        for value in rows[1:]:
            right = mu * right + value
        left = rows[-1]
        for value in rows[-2::-1]:
            left = mu * left + value
        return right, left, rows

    def weigh(block, _):
        right, left, _ = sums(block, tile(block))
        pay_ref[block, 0] = right
        pay_ref[block, 1] = left
        return 0

    lax.fori_loop(1, NX // ROWS, weigh, 0, unroll=8)
    right, left, rows = sums(0, tile(0))
    moment0 = functools.reduce(jnp.add, rows)
    moment1 = functools.reduce(jnp.add, [float(r - 1) * rows[r] for r in range(EXT) if r != 1])
    pay_ref[0, 0] = jnp.where(origin, moment0, right)
    pay_ref[0, 1] = jnp.where(origin, moment1, left)
    wait_all(copies)


def far_kernel(pay_ref, step_ref, wrap_ref, out_ref):
    slab = lax.axis_index("slab")
    step = step_ref[tile(slab), :]
    wrap = wrap_ref[tile(slab), :]
    row, lane = iotas()
    origin = (row == 0) & (lane == 0) & (slab == 0)
    right = jnp.zeros((ROWS, NZ), jnp.float32)
    left = right
    total0 = right
    total1 = right
    ramp = right
    for s in range(SLABS):
        right = step * right + pay_ref[s, 0]
        left = step * left + pay_ref[SLABS - 1 - s, 1]
        total0 = total0 + pay_ref[s, 0]
        total1 = total1 + pay_ref[s, 1]
        ramp = ramp + float((SLABS - s) % SLABS) * pay_ref[s, 0]
    right = right * wrap
    left = left * wrap
    for s in range(SLABS):
        m0, m1 = pay_ref[s, 0], pay_ref[s, 1]
        if s:
            ramp = ramp + total0 - float(SLABS) * m0
        slope = 0.5 * (total0 - m0) - (ROWS / NY) * ramp + (1.0 / NY) * (total1 - m1)
        out_ref[s, 0] = jnp.where(origin, slope, right)
        right = step * right + m0
        t = SLABS - 1 - s
        curve = (-0.5 / NY) * (total0 - pay_ref[t, 0])
        out_ref[t, 1] = jnp.where(origin, curve, left)
        left = step * left + pay_ref[t, 1]


OUT_CHUNKS = 4
HAT_CHUNKS = 2


def green0(j):
    return 0.5 * j - j * j / (2.0 * NY)


def final_kernel(
    ret_ref, prev_ref, next_ref, store,
    out_hbm, press, field, rim, out_ref, field_ref, hat_ref, table_ref, sems, out_sems,
):
    part = NX // HAT_CHUNKS
    hats = []
    for k in range(HAT_CHUNKS):
        hats += [(store.at[pl.ds(STORE_HAT + r * NX + k * part, part)], hat_ref.at[r, pl.ds(k * part, part)]) for r in range(EXT)]
    lines = (pl.ds(0, NX), pl.ds(NX, LATER - NX))
    later = [(store.at[pl.ds(STORE_LATER + s.start, s.size)], table_ref.at[s]) for s in lines]
    fields = [(store.at[pl.ds(c * CELLS, CELLS)], field_ref.at[c]) for c in range(3)]
    copies = start_all([later[0], *hats, later[1], *fields], sems)
    wait_all(copies[: 1 + EXT])
    copies = copies[1 + EXT :]
    row, lane = iotas()
    first_row, last_row = row == 0, row == ROWS - 1
    first_lane, last_lane = lane == 0, lane == NZ - 1
    origin = (row == 0) & (lane == 0)

    def solve(block, at):
        mu = table_ref[at, :]
        inv = 1.0 / jnp.where(mu == 0.0, 1.0, mu)
        scale = jnp.where(mu == 0.0, 0.0, -1.0 / ((1.0 + mu) * (1.0 - mu) * inv))
        rows = [hat_ref[r, at, :] for r in range(EXT)]
        below = [ret_ref[block, 0] * inv + rows[0]]
        for value in rows[1:]:
            below.append(mu * below[-1] + value)
        above = [ret_ref[block, 1] * inv]
        for value in rows[:0:-1]:
            above.append(mu * (above[-1] + value))
        above.reverse()
        return [scale * (a + b) for a, b in zip(below, above)], rows

    def line(block, _):
        at = tile(block)
        values, _ = solve(block, at)
        for r in range(EXT):
            press[r, at, :] = values[r]
        return 0

    count = part // ROWS
    for k in range(HAT_CHUNKS):
        if k:
            wait_all(copies[:EXT])
            copies = copies[EXT:]
        lax.fori_loop(k * count, (k + 1) * count, line, 0, unroll=8)
    at = pl.ds(0, ROWS)
    values, rows = solve(0, at)
    slope, curve = ret_ref[0, 0], ret_ref[0, 1]
    for r in range(EXT):
        y = float(r - 1)
        mean_line = slope * y + curve * (y * y)
        for k in range(EXT):
            if k != r:
                mean_line = mean_line + green0(float(abs(r - k))) * rows[k]
        press[r, at, :] = jnp.where(origin, mean_line, values[r])

    copies[0].wait()
    x_high, x_low = parts(x_matrix(table_ref))
    z_high, z_low = parts(twice(table_ref[pl.ds(TAB_Z, NZ), :]))
    for r in range(0, EXT, 2):
        pair = jnp.concatenate([press[r], press[r + 1]], 1)
        both = dot3(*parts(dot3(x_high, x_low, *parts(pair))), z_high, z_low)
        for k, plane in zip((r, r + 1), halves(both)):
            if k == 0:
                rim[every8(0), :] = plane - 0.5 * prev_ref[...]
            elif k == EXT - 1:
                rim[every8(ROWS - 1), :] = plane + 0.5 * next_ref[...]
            else:
                field[every8(k - 1), :] = plane

    def project(x, carry):
        behind, now = carry
        ahead = field[tile(lax.rem(x + 1, NX)), :]
        edge = rim[tile(x), :]
        up = jnp.where(last_row, edge, pltpu.roll(now, ROWS - 1, 0))
        down = jnp.where(first_row, edge, pltpu.roll(now, 1, 0))
        grads = (ahead - behind, up - down, centred_z(now, first_lane, last_lane))
        for c in range(3):
            out_ref[c, tile(x), :] = field_ref[c, tile(x), :] - 0.5 * grads[c]
        return now, ahead

    carry = (field[tile(NX - 1), :], field[tile(0), :])
    wait_all(copies[1:])
    copies = []
    part = CELLS // OUT_CHUNKS
    count = NX // OUT_CHUNKS
    for k in range(OUT_CHUNKS):
        carry = lax.fori_loop(k * count, (k + 1) * count, project, carry, unroll=32)
        rows = pl.ds(k * part, part)
        copies.append(pltpu.make_async_copy(out_ref.at[:, rows], out_hbm.at[:, rows], out_sems.at[k]))
        copies[-1].start()
    wait_all(copies)


def pick_kernel(which, count, *refs):
    *pieces, out_ref = refs[: count] + refs[-1:]
    me = lax.axis_index("sim")
    for k, piece in enumerate(pieces):

        @pl.when(which(me) == k)
        def _(piece=piece):
            out_ref[...] = piece[...]


def pick(name, which, pieces, *after):
    (out,) = call(
        functools.partial(pick_kernel, which, len(pieces)),
        [pieces[0].shape],
        name,
        in_specs=[VM] * len(pieces) + [HB] * len(after),
        nbytes=2**18,
    )(*pieces, *after)
    return out


def scatter_y(piece):
    came = [lax.ppermute(piece[k], "sim", [(0, k)]) for k in (1, 2, 3)]
    return pick("pick_y", lambda me: lax.rem(me, 4), [piece[0], *came])


def gather_y(mine):
    quarters = [mine]
    for k in (1, 2, 3):
        pairs = [(4 * z + i, 4 * z + (i + k) % 4) for z in range(2) for i in range(4)]
        quarters.append(lax.ppermute(mine, "sim", pairs))
    return quarters


def local(velocity, viscosity, turbines, fringe_start):
    vel = velocity.reshape(3, CELLS, NZ)
    visc = viscosity.reshape(CELLS, NZ)
    turb = turbines.reshape(CELLS, NZ)
    x_basis = x_table()[0]
    z_basis = z_table()
    mu, step, wrap = line_tables()
    table, later = (
        np.concatenate([mu, x[:, :NZ], x[:, NZ:], z]).astype(np.float32)
        for x, z in ((x_basis, z_basis.T), (x_basis.T, z_basis))
    )
    around = np.arange(-ROWS, NX + ROWS) % NX
    near = x_basis.T[around]
    near_table = np.concatenate([mu, z_basis.T, near[:, :NZ], near[:, NZ:]]).astype(np.float32)
    profile = (np.sin(math.pi * (np.arange(FR) + 0.5) / FR) ** 2).astype(np.float32)
    upward = [(i, (i + 1) % SLABS) for i in range(SLABS)]
    downward = [((i + 1) % SLABS, i) for i in range(SLABS)]

    f32 = jnp.float32
    quarter = (3 * FR * ROWS // 4, NZ)
    plane = (NX, NZ)
    *pieces, low, high = call(
        edges_kernel,
        [quarter] * 4 + [(4, NX, NZ)] * 2,
        "edges",
        room=60,
        in_specs=[SM, HB, HB],
        out_specs=[HB] * 6,
        scratch=[
            pltpu.VMEM((3, CELLS, NZ), f32),
            pltpu.VMEM((CELLS, NZ), f32),
            pltpu.VMEM((4, NX, NZ), f32),
            pltpu.VMEM((4, NX, NZ), f32),
            pltpu.SemaphoreType.DMA((2 * EDGE_CHUNKS,)),
            pltpu.SemaphoreType.DMA((2 * EDGE_CHUNKS,)),
            pltpu.SemaphoreType.DMA((6,)),
        ],
        nbytes=6 * 2**20,
    )(fringe_start, vel, visc)
    prev = lax.ppermute(high, "slab", upward)
    following = lax.ppermute(low, "slab", downward)

    mine = scatter_y(pieces)
    came = lax.ppermute(mine, "sim", [(i, i + 4) for i in range(4)])
    fields, done = call(
        diffuse_kernel,
        [(3, CELLS, NZ), (ROWS, NZ)],
        "diffuse",
        room=DIFFUSE_ROOM,
        in_specs=[VM] * 2 + [HB],
        flops=2**26,
        nbytes=8 * 2**20,
    )(vel, visc, mine)
    quarters = gather_y(pick("pick_z", lambda me: me // 4, [mine, came], done))
    store, hat, v_low, v_high, _ = call(
        forward_kernel,
        [(STORE, NZ), (EXT, NX, NZ), plane, plane, (3, CELLS, NZ)],
        "forward",
        room=FORWARD_ROOM,
        in_specs=[SM] + [VM] * 2 + [HB] * 5 + [SM] + [VM] * 2,
        out_specs=[HB, VM, VM, VM, VM],
        scratch=[
            pltpu.VMEM((4, 4, NX, NZ), f32),
            pltpu.VMEM((CELLS, NZ), f32),
            pltpu.VMEM((CELLS, NZ), f32),
            pltpu.SemaphoreType.DMA((4,)),
            pltpu.SemaphoreType.DMA((4,)),
        ],
        flops=2**30,
        nbytes=10 * 2**20,
        input_output_aliases={1: 4},
    )(fringe_start, fields, turb, low, high, prev, following, quarters[0], profile, table, later)
    store, pay, v_low, v_high = call(
        precursor_kernel,
        [(STORE, NZ), (SLABS, 2, ROWS, NZ), plane, plane],
        "precursor",
        room=FORWARD_ROOM,
        in_specs=[SM] + [VM] * 4 + [SM] + [VM] * 4 + [HB],
        out_specs=[HB, VM, VM, VM],
        scratch=[
            pltpu.VMEM((3 * FR * ROWS, NZ), f32),
            pltpu.VMEM((3, (WINDOW + 2) * ROWS, NZ), f32),
            pltpu.VMEM((WINDOW * ROWS, NZ), f32),
            pltpu.VMEM((WINDOW * ROWS, NZ), f32),
            pltpu.VMEM((3, FR * ROWS, NZ), f32),
            pltpu.VMEM((NX + ROWS, NZ), f32),
            pltpu.VMEM((EXT, NX, NZ), f32),
            pltpu.SemaphoreType.DMA((EXT + 3,)),
            pltpu.SemaphoreType.DMA((3,)),
        ],
        flops=2**28,
        nbytes=3 * 2**20,
        input_output_aliases={10: 0},
    )(fringe_start, *quarters, profile, hat, v_low, v_high, near_table, store)
    v_prev = lax.ppermute(v_high, "slab", upward)
    v_next = lax.ppermute(v_low, "slab", downward)
    pay = lax.all_to_all(pay, "slab", split_axis=0, concat_axis=0, tiled=True)
    (ret,) = call(
        far_kernel,
        [(SLABS, 2, ROWS, NZ)],
        "far",
        in_specs=[VM] * 3,
        nbytes=2**19,
    )(pay, step, wrap)
    ret = lax.all_to_all(ret, "slab", split_axis=0, concat_axis=0, tiled=True)
    (out,) = call(
        final_kernel,
        [(3, CELLS, NZ)],
        "final",
        room=FORWARD_ROOM,
        in_specs=[VM, VM, VM, HB],
        out_specs=[HB],
        scratch=[
            pltpu.VMEM((EXT, NX, NZ), f32),
            pltpu.VMEM((CELLS, NZ), f32),
            pltpu.VMEM((CELLS, NZ), f32),
            pltpu.VMEM((3, CELLS, NZ), f32),
            pltpu.VMEM((3, CELLS, NZ), f32),
            pltpu.VMEM((EXT, NX, NZ), f32),
            pltpu.VMEM((LATER, NZ), f32),
            pltpu.SemaphoreType.DMA((5 + HAT_CHUNKS * EXT,)),
            pltpu.SemaphoreType.DMA((OUT_CHUNKS,)),
        ],
        flops=2**30,
        nbytes=10 * 2**20,
    )(ret, v_prev, v_next, store)
    return out.reshape(velocity.shape)


def solution(mesh):
    return jax.shard_map(
        local,
        mesh=mesh,
        in_specs=(
            P("sim", None, None, "slab", None),
            P("sim", None, "slab", None),
            P("sim", None, "slab", None),
            P(),
        ),
        out_specs=P("sim", None, None, "slab", None),
        check_vma=False,
    )
```
